32 devices in a mesh: layer: 8 (over y, x, core), batch: 4 (over z).
Axes of the slice: x: 2, y: 2, z: 4, core: 2. Of those that a mesh axis runs over, the one named last changes fastest.
Arguments:
- images: bfloat16 [32, 4, 4, 512], P('batch'), parts along dimension 0, may hold values from -6 to 6
- weights: bfloat16 [16, 4608, 512], P('layer'), may hold values from -0.25 to 0.25
- biases: float32 [16, 512], P('layer'), may hold values from -3 to 3
Outputs:
- states: float32 [16, 32, 4, 4, 512], P('layer', 'batch'), parts along dimension 1
The draws below stay inside these ranges and needn't reach their ends.
There are 4 independent parts, one for each index of `batch`. The reference program is written for one: setup_inputs(seed, part) draws one part's arguments, and reference() takes and returns one part's arrays. A program takes and returns all parts, laid end to end along the dimension named above; an argument that names none is the same for every part. Nothing has to cross between parts.
All inputs are finite; a program needn't handle non-finite values.
Results may differ from the reference program's by a relative error of at most 0.015.
Values sent between devices are 32-bit elements; how exact they have to be, the bound alone decides.
A program may use at most 64 MiB of HBM per device.

```python
import jax
import jax.numpy as jnp
from jax import lax

C = 512
MAP = 4
IMG = 8
LAYERS = 16


def level_of(own_key, dims, shards, low, largest):
    def one(axis_at, parts):
        draws = jax.random.uniform(jax.random.fold_in(jax.random.fold_in(own_key, 6), axis_at), (parts,), jnp.float32, low / len(shards), largest / len(shards))
        return jnp.repeat(jnp.exp(draws), dims[axis_at] // parts).reshape((-1,) + (1,) * (len(dims) - axis_at - 1))

    factor_of = one(*shards[0])
    for cut in shards[1:]:
        factor_of = factor_of * one(*cut)
    return factor_of


def bell_draw(rng, dims, spread, most, cuts=(), held_as=jnp.bfloat16):
    array = spread * jax.random.normal(rng, dims, jnp.float32)
    if cuts:
        array = array * level_of(rng, dims, cuts, -0.22, 0.18)
    return jnp.clip(array, -most, most).astype(held_as)


def setup_inputs(seed: int = 0, part: int = 0) -> dict:
    keys = jax.random.split(jax.random.key(seed), 4)
    part_splits = jax.random.split(jax.random.fold_in(keys[3], part), 4)
    images = bell_draw(part_splits[0], (IMG, MAP, MAP, C), 1.0, 6.0)
    weights = bell_draw(keys[1], (LAYERS, 9 * C, C), C ** -0.5, 0.25, ((0, 8),))
    biases = bell_draw(keys[2], (LAYERS, C), 0.5, 3.0, ((0, 8),), jnp.float32)
    return {"images": images, "weights": weights, "biases": biases}


step_size = 0.25


def fine_step(field, weight, bias):
    channels = field.shape[-1]
    height = field.shape[1]
    breadth = field.shape[2]
    lowered = field.astype(jnp.bfloat16)
    padded = jnp.pad(lowered, ((0, 0), (1, 1), (1, 1), (0, 0)))
    pieces = [padded[:, row_shift:row_shift + height, col_shift:col_shift + breadth, :] for row_shift in range(3) for col_shift in range(3)]
    stacked = jnp.concatenate(pieces, axis=-1).reshape(-1, 9 * channels)
    mixed = jnp.dot(stacked, weight, preferred_element_type=jnp.float32).reshape(field.shape) + bias
    return field + step_size * jnp.tanh(mixed)


def coarse_step(field, weight, bias):
    channels = field.shape[-1]
    lowered = field.astype(jnp.bfloat16).reshape(-1, channels)
    centre = weight[4 * channels:5 * channels]
    mixed = jnp.dot(lowered, centre, preferred_element_type=jnp.float32).reshape(field.shape) + bias
    return field + 2.0 * step_size * jnp.tanh(mixed)


def reference(images, weights, biases):
    channels = images.shape[-1]
    blocks = weights.shape[0] // 2
    block_weights = weights.reshape(blocks, 2, 9 * channels, channels)
    block_biases = biases.reshape(blocks, 2, channels)
    initial = images.astype(jnp.float32)

    def relax_block(pair):
        kernel, offset_bias = pair
        return fine_step(fine_step(initial, kernel[0], offset_bias[0]), kernel[1], offset_bias[1])

    guessed = lax.map(relax_block, (block_weights, block_biases))
    shifted = jnp.concatenate([initial[None], guessed[:-1]], axis=0)

    def forcing_block(triple):
        begin, kernel, offset_bias = triple
        relaxed = fine_step(begin, kernel[0], offset_bias[0])
        return fine_step(relaxed, kernel[1], offset_bias[1]) - coarse_step(begin, kernel[0], offset_bias[0])

    forcing = lax.map(forcing_block, (shifted, block_weights, block_biases))

    def chain_step(current, triple):
        extra, kernel, offset_bias = triple
        following = coarse_step(current, kernel[0], offset_bias[0]) + extra
        return following, following

    _, coarse = lax.scan(chain_step, initial, (forcing, block_weights, block_biases))
    predecessors = jnp.concatenate([initial[None], coarse[:-1]], axis=0)

    def finish_block(triple):
        begin, kernel, offset_bias = triple
        return fine_step(begin, kernel[0], offset_bias[0])

    finished = lax.map(finish_block, (predecessors, block_weights, block_biases))
    states = jnp.stack([finished, coarse], axis=1)
    return states.reshape((weights.shape[0],) + initial.shape)
```

```python
import functools

import jax
import jax.numpy as jnp
from jax import lax
from jax.experimental import pallas as pl
from jax.experimental.pallas import tpu as pltpu
from jax.sharding import PartitionSpec as P

MESH = pl.DeviceIdType.MESH
step_size = 0.25


def dot(a, b):
    return jnp.dot(a, b, preferred_element_type=jnp.float32)


def kernel(
    n,
    img_ref,
    w_hbm,
    b_ref,
    out_ref,
    wv,
    pad,
    cols,
    gsend,
    shifted,
    crecv,
    w_sem,
    gs_sem,
    gr_sem,
    cs_sem,
    cr_sem,
):
    me = lax.axis_index("layer")
    right, left = lax.rem(me + 1, n), lax.rem(me + n - 1, n)
    side, images, channels = img_ref.shape[0], img_ref.shape[2], img_ref.shape[3]
    half = channels // 2
    rows = side * side * images
    has_next = me < n - 1

    def load(l, h):
        return pltpu.make_async_copy(w_hbm.at[l, :, h], wv.at[l, :, h], w_sem.at[l, h])

    for l in range(2):
        for h in range(2):
            load(l, h).start()

    barrier = pltpu.get_barrier_semaphore()
    for neighbour in (left, right):
        pl.semaphore_signal(
            barrier, inc=1, device_id={"layer": neighbour}, device_id_type=MESH
        )

    def send_guess(q):
        return pltpu.make_async_remote_copy(
            src_ref=gsend.at[q],
            dst_ref=shifted.at[q],
            send_sem=gs_sem.at[q],
            recv_sem=gr_sem.at[q],
            device_id={"layer": right},
            device_id_type=MESH,
        )

    def send_coarse(g):
        return pltpu.make_async_remote_copy(
            src_ref=out_ref.at[1, g],
            dst_ref=crecv.at[g],
            send_sem=cs_sem.at[g],
            recv_sem=cr_sem.at[g],
            device_id={"layer": right},
            device_id_type=MESH,
        )

    def cut(h):
        return slice(h * half, (h + 1) * half)

    def build(h):
        for tap in range(9):
            dy, dx = tap // 3, tap % 3
            piece = pad[dy : dy + side, dx : dx + side, :, cut(h)]
            cols[h, :, tap * half : (tap + 1) * half] = piece.reshape(rows, half).astype(
                jnp.bfloat16
            )

    def weight(l, h, q):
        return wv[l, :, h, :, cut(q)].reshape(9 * half, half)

    def fine(l, before, emit):
        before(0)
        build(0)
        parts = [dot(cols[0], weight(l, 0, q)) for q in range(2)]
        before(1)
        build(1)
        for q in range(2):
            mixed = parts[q] + dot(cols[1], weight(l, 1, q)) + b_ref[l : l + 1, cut(q)]
            base = pad[1 : 1 + side, 1 : 1 + side, :, cut(q)].reshape(rows, half)
            emit(q, base + step_size * jnp.tanh(mixed))

    def grid_of(value):
        return value.reshape(side, side, images, value.shape[-1])

    def to_pad(q, value):
        pad[1 : 1 + side, 1 : 1 + side, :, cut(q)] = grid_of(value)

    def coarse(field, bias):
        centre = wv[0, 4].reshape(channels, channels)
        mixed = dot(field.astype(jnp.bfloat16), centre) + bias
        return field + 2.0 * step_size * jnp.tanh(mixed)

    def no_wait(h):
        pass

    pad[...] = jnp.zeros_like(pad)
    pad[1 : 1 + side, 1 : 1 + side] = img_ref[...].astype(jnp.float32)
    fine(0, lambda h: load(0, h).wait(), to_pad)

    @pl.when(me == 0)
    def _():
        out_ref[0] = pad[1 : 1 + side, 1 : 1 + side]

    pl.semaphore_wait(barrier, 2)

    def emit_guess(q, value):
        gsend[q] = value

        @pl.when(has_next)
        def _():
            send_guess(q).start()

    fine(1, lambda h: load(1, h).wait(), emit_guess)

    @pl.when(me == 0)
    def _():
        for q in range(2):
            out_ref[1, :, :, :, cut(q)] = grid_of(gsend[q])

    @pl.when(me >= 1)
    def _():
        def arrive(h):
            send_guess(h).wait_recv()
            to_pad(h, shifted[h])

        fine(0, arrive, to_pad)

        @pl.when(me == 1)
        def _():
            out_ref[0] = pad[1 : 1 + side, 1 : 1 + side]

        def emit_end(q, value):
            out_ref[1, :, :, :, cut(q)] = grid_of(value)

        fine(1, no_wait, emit_end)

        @pl.when((me == 1) & has_next)
        def _():
            for g in range(side):
                send_coarse(g).start()

    @pl.when(me >= 2)
    def _():
        bias = b_ref[0:1, :]
        start = jnp.concatenate([shifted[0], shifted[1]], axis=1)
        out_ref[1] = out_ref[1] - grid_of(coarse(start, bias))
        for g in range(side):
            send_coarse(g).wait_recv()
            field = crecv[g].reshape(side * images, channels)
            solved = coarse(field, bias).reshape(side, images, channels)
            out_ref[1, g] = solved + out_ref[1, g]

            @pl.when(has_next)
            def _():
                send_coarse(g).start()

            pad[1 + g, 1 : 1 + side] = crecv[g]

        def emit_finished(q, value):
            out_ref[0, :, :, :, cut(q)] = grid_of(value)

        fine(0, no_wait, emit_finished)

    @pl.when(has_next)
    def _():
        for q in range(2):
            send_guess(q).wait_send()

    @pl.when((me >= 1) & has_next)
    def _():
        for g in range(side):
            send_coarse(g).wait_send()


def shards(n, images, weights, biases):
    count, side, _, channels = images.shape
    half = channels // 2
    rows = side * side * count
    field = jnp.transpose(images, (1, 2, 0, 3))
    taps = weights.reshape(2, 9, 2, half, channels)
    vmem = pl.BlockSpec(memory_space=pltpu.VMEM)
    f32, bf16 = jnp.float32, jnp.bfloat16
    out = pl.pallas_call(
        functools.partial(kernel, n),
        out_shape=jax.ShapeDtypeStruct((2, side, side, count, channels), f32),
        in_specs=[vmem, pl.BlockSpec(memory_space=pl.ANY), vmem],
        out_specs=vmem,
        scratch_shapes=[
            pltpu.VMEM(taps.shape, bf16),
            pltpu.VMEM((side + 2, side + 2, count, channels), f32),
            pltpu.VMEM((2, rows, 9 * half), bf16),
            pltpu.VMEM((2, rows, half), f32),
            pltpu.VMEM((2, rows, half), f32),
            pltpu.VMEM((side, side, count, channels), f32),
            pltpu.SemaphoreType.DMA((2, 2)),
            pltpu.SemaphoreType.DMA((2,)),
            pltpu.SemaphoreType.DMA((2,)),
            pltpu.SemaphoreType.DMA((side,)),
            pltpu.SemaphoreType.DMA((side,)),
        ],
        compiler_params=pltpu.CompilerParams(
            collective_id=0, has_side_effects=True, vmem_limit_bytes=56 * 2**20
        ),
    )(field, taps, biases)
    return jnp.transpose(out, (0, 3, 1, 2, 4))


def solution(mesh):
    return jax.shard_map(
        functools.partial(shards, mesh.shape["layer"]),
        mesh=mesh,
        in_specs=(P("batch", None, None, None), P("layer", None, None), P("layer", None)),
        out_specs=P("layer", "batch", None, None, None),
        check_vma=False,
    )
```

```python
import functools

import jax
import jax.numpy as jnp
from jax import lax
from jax.experimental import pallas as pl
from jax.experimental.pallas import tpu as pltpu
from jax.sharding import PartitionSpec as P

MESH = pl.DeviceIdType.MESH
step_size = 0.25


def dot(a, b):
    return jnp.dot(a, b, preferred_element_type=jnp.float32)


def kernel(
    n,
    img_ref,
    w_hbm,
    b_ref,
    out_ref,
    wv,
    pad,
    cols,
    gsend,
    shifted,
    crecv,
    stage,
    w_sem,
    gs_sem,
    gr_sem,
    cs_sem,
    cr_sem,
):
    me = lax.axis_index("layer")
    right, left = lax.rem(me + 1, n), lax.rem(me + n - 1, n)
    images, side, _, channels = img_ref.shape
    half = channels // 2
    rows = side * side * images
    has_next = me < n - 1

    def loads(l, h):
        return [
            pltpu.make_async_copy(
                w_hbm.at[l, 3 * r : 3 * r + 3, h],
                wv.at[l, 3 * r : 3 * r + 3, h],
                w_sem.at[l, h, r],
            )
            for r in range(3)
        ]

    def start_load(l, h):
        for copy in loads(l, h):
            copy.start()

    def wait_load(l, h):
        for copy in loads(l, h):
            copy.wait()

    start_load(0, 0)
    start_load(0, 1)

    barrier = pltpu.get_barrier_semaphore()
    for neighbour in (left, right):
        pl.semaphore_signal(
            barrier, inc=1, device_id={"layer": neighbour}, device_id_type=MESH
        )

    def send_guess(q):
        return pltpu.make_async_remote_copy(
            src_ref=gsend.at[q],
            dst_ref=shifted.at[q],
            send_sem=gs_sem.at[q],
            recv_sem=gr_sem.at[q],
            device_id={"layer": right},
            device_id_type=MESH,
        )

    def send_coarse(g):
        return pltpu.make_async_remote_copy(
            src_ref=out_ref.at[1, g],
            dst_ref=crecv.at[g],
            send_sem=cs_sem.at[g],
            recv_sem=cr_sem.at[g],
            device_id={"layer": right},
            device_id_type=MESH,
        )

    def cut(h):
        return slice(h * half, (h + 1) * half)

    def build(h):
        for tap in range(9):
            dy, dx = tap // 3, tap % 3
            piece = pad[dy : dy + side, dx : dx + side, :, cut(h)]
            cols[h, :, tap * half : (tap + 1) * half] = piece.reshape(rows, half).astype(
                jnp.bfloat16
            )

    def weight(l, h, q):
        return wv[l, :, h, :, cut(q)].reshape(9 * half, half)

    def fine(l, before, emit):
        before(0)
        build(0)
        parts = [dot(cols[0], weight(l, 0, q)) for q in range(2)]
        before(1)
        build(1)
        for q in range(2):
            mixed = parts[q] + dot(cols[1], weight(l, 1, q)) + b_ref[l : l + 1, cut(q)]
            base = pad[1 : 1 + side, 1 : 1 + side, :, cut(q)].reshape(rows, half)
            emit(q, base + step_size * jnp.tanh(mixed))

    def grid_of(value):
        return value.reshape(side, side, images, value.shape[-1])

    def to_pad(q, value):
        pad[1 : 1 + side, 1 : 1 + side, :, cut(q)] = grid_of(value)

    def coarse(field, bias):
        centre = wv[0, 4].reshape(channels, channels)
        mixed = dot(field.astype(jnp.bfloat16), centre) + bias
        return field + 2.0 * step_size * jnp.tanh(mixed)

    def no_wait(h):
        pass

    pad[...] = jnp.zeros_like(pad)
    lanes = 128
    tiles = channels // lanes
    for m in range(images):
        for i in range(side):
            row = img_ref[m, i].astype(jnp.float32)
            for c in range(tiles):
                at = ((m * side + i) * tiles + c) * side
                stage[at : at + side, :] = row[:, c * lanes : (c + 1) * lanes]
    for i in range(side):
        for c in range(tiles):
            for j in range(side):
                at = (i * tiles + c) * side + j
                pad[1 + i, 1 + j, :, c * lanes : (c + 1) * lanes] = stage[
                    pl.ds(at, images, stride=side * tiles * side), :
                ]

    def first_layer(h):
        wait_load(0, h)
        start_load(1, h)

    fine(0, first_layer, to_pad)

    @pl.when(me == 0)
    def _():
        out_ref[0] = pad[1 : 1 + side, 1 : 1 + side]

    pl.semaphore_wait(barrier, 2)

    def emit_guess(q, value):
        gsend[q] = value

        @pl.when(has_next)
        def _():
            send_guess(q).start()

    fine(1, lambda h: wait_load(1, h), emit_guess)

    @pl.when(me == 0)
    def _():
        for q in range(2):
            out_ref[1, :, :, :, cut(q)] = grid_of(gsend[q])

    @pl.when(me >= 1)
    def _():
        def arrive(h):
            send_guess(h).wait_recv()
            to_pad(h, shifted[h])

        fine(0, arrive, to_pad)

        @pl.when(me == 1)
        def _():
            out_ref[0] = pad[1 : 1 + side, 1 : 1 + side]

        def emit_end(q, value):
            out_ref[1, :, :, :, cut(q)] = grid_of(value)

        fine(1, no_wait, emit_end)

        @pl.when((me == 1) & has_next)
        def _():
            for g in range(side):
                send_coarse(g).start()

    @pl.when(me >= 2)
    def _():
        bias = b_ref[0:1, :]
        start = jnp.concatenate([shifted[0], shifted[1]], axis=1)
        out_ref[1] = out_ref[1] - grid_of(coarse(start, bias))
        for g in range(side):
            send_coarse(g).wait_recv()
            field = crecv[g].reshape(side * images, channels)
            solved = coarse(field, bias).reshape(side, images, channels)
            out_ref[1, g] = solved + out_ref[1, g]

            @pl.when(has_next)
            def _():
                send_coarse(g).start()

            pad[1 + g, 1 : 1 + side] = crecv[g]

        def emit_finished(q, value):
            out_ref[0, :, :, :, cut(q)] = grid_of(value)

        fine(0, no_wait, emit_finished)

    @pl.when(has_next)
    def _():
        for q in range(2):
            send_guess(q).wait_send()

    @pl.when((me >= 1) & has_next)
    def _():
        for g in range(side):
            send_coarse(g).wait_send()


def shards(n, images, weights, biases):
    count, side, _, channels = images.shape
    half = channels // 2
    rows = side * side * count
    taps = weights.reshape(2, 9, 2, half, channels)
    vmem = pl.BlockSpec(memory_space=pltpu.VMEM)
    f32, bf16 = jnp.float32, jnp.bfloat16
    out = pl.pallas_call(
        functools.partial(kernel, n),
        out_shape=jax.ShapeDtypeStruct((2, side, side, count, channels), f32),
        in_specs=[vmem, pl.BlockSpec(memory_space=pl.ANY), vmem],
        out_specs=vmem,
        scratch_shapes=[
            pltpu.VMEM(taps.shape, bf16),
            pltpu.VMEM((side + 2, side + 2, count, channels), f32),
            pltpu.VMEM((2, rows, 9 * half), bf16),
            pltpu.VMEM((2, rows, half), f32),
            pltpu.VMEM((2, rows, half), f32),
            pltpu.VMEM((side, side, count, channels), f32),
            pltpu.VMEM((rows * channels // 128, 128), f32),
            pltpu.SemaphoreType.DMA((2, 2, 3)),
            pltpu.SemaphoreType.DMA((2,)),
            pltpu.SemaphoreType.DMA((2,)),
            pltpu.SemaphoreType.DMA((side,)),
            pltpu.SemaphoreType.DMA((side,)),
        ],
        compiler_params=pltpu.CompilerParams(
            collective_id=0, has_side_effects=True, vmem_limit_bytes=56 * 2**20
        ),
    )(images, taps, biases)
    return jnp.transpose(out, (0, 3, 1, 2, 4))


def solution(mesh):
    return jax.shard_map(
        functools.partial(shards, mesh.shape["layer"]),
        mesh=mesh,
        in_specs=(P("batch", None, None, None), P("layer", None, None), P("layer", None)),
        out_specs=P("layer", "batch", None, None, None),
        check_vma=False,
    )
```

```python
import functools

import jax
import jax.numpy as jnp
from jax import lax
from jax.experimental import pallas as pl
from jax.experimental.pallas import tpu as pltpu
from jax.sharding import PartitionSpec as P

MESH = pl.DeviceIdType.MESH
step_size = 0.25


def dot(a, b):
    return jnp.dot(a, b, preferred_element_type=jnp.float32)


def kernel(
    n,
    img_ref,
    w_hbm,
    b_ref,
    out_ref,
    wv,
    pad,
    cols,
    gsend,
    shifted,
    stage,
    force,
    wsend,
    wrecv,
    wc,
    bc,
    fo,
    cin,
    abuf,
    bbuf,
    peer_fin,
    peer_out,
    w_sem,
    g_sem,
    wx_sem,
    fx_sem,
    cs_sem,
    cr_sem,
    pf_sem,
    po_sem,
):
    me = lax.axis_index("layer")
    right, left = lax.rem(me + 1, n), lax.rem(me + n - 1, n)
    images, side, _, channels = img_ref.shape
    half = channels // 2
    rows = side * side * images
    has_next = me < n - 1
    has_next_pair = me < n - 2
    core = lax.rem(me, 2)
    other = 1 - core
    partner = me + 1 - 2 * core
    ahead, behind = lax.rem(me + 2, n), lax.rem(me + n - 2, n)
    groups = side // 2

    def loads(l, h):
        return [
            pltpu.make_async_copy(
                w_hbm.at[l, 3 * r : 3 * r + 3, h],
                wv.at[l, 3 * r : 3 * r + 3, h],
                w_sem.at[l, h, r],
            )
            for r in range(3)
        ]

    def start_load(l, h):
        for copy in loads(l, h):
            copy.start()

    def wait_load(l, h):
        for copy in loads(l, h):
            copy.wait()

    start_load(0, 0)
    start_load(0, 1)

    barrier = pltpu.get_barrier_semaphore()
    for neighbour in (left, right, behind, ahead):
        pl.semaphore_signal(
            barrier, inc=1, device_id={"layer": neighbour}, device_id_type=MESH
        )

    def remote(src, dst, send_sem, recv_sem, target):
        return pltpu.make_async_remote_copy(
            src_ref=src,
            dst_ref=dst,
            send_sem=send_sem,
            recv_sem=recv_sem,
            device_id={"layer": target},
            device_id_type=MESH,
        )

    def send_guess(q):
        return remote(gsend.at[q], shifted.at[q], g_sem.at[0, q], g_sem.at[1, q], right)

    def send_centre():
        return remote(wsend, wrecv, wx_sem.at[0], wx_sem.at[1], partner)

    def send_force():
        away = force.at[pl.ds(groups * other, groups)]
        return remote(away, fo.at[core], fx_sem.at[0], fx_sem.at[1], partner)

    def first_coarse(t, g):
        src = out_ref.at[1, groups * t + g]
        return remote(src, cin.at[g], cs_sem.at[t, g], cr_sem.at[g], me + 1 + t)

    def send_coarse(g):
        return remote(bbuf.at[g], cin.at[g], cs_sem.at[0, g], cr_sem.at[g], ahead)

    def send_fin(src, g):
        return remote(src.at[g], peer_fin.at[g], pf_sem.at[0, g], pf_sem.at[1, g], partner)

    def send_out(src, g):
        return remote(src.at[g], peer_out.at[g], po_sem.at[0, g], po_sem.at[1, g], partner)

    def cut(h):
        return slice(h * half, (h + 1) * half)

    def build(h):
        for tap in range(9):
            dy, dx = tap // 3, tap % 3
            piece = pad[dy : dy + side, dx : dx + side, :, cut(h)]
            cols[h, :, tap * half : (tap + 1) * half] = piece.reshape(rows, half).astype(
                jnp.bfloat16
            )

    def weight(l, h, q):
        return wv[l, :, h, :, cut(q)].reshape(9 * half, half)

    def fine(l, before, emit):
        before(0)
        build(0)
        parts = [dot(cols[0], weight(l, 0, q)) for q in range(2)]
        before(1)
        build(1)
        for q in range(2):
            mixed = parts[q] + dot(cols[1], weight(l, 1, q)) + b_ref[l : l + 1, cut(q)]
            base = pad[1 : 1 + side, 1 : 1 + side, :, cut(q)].reshape(rows, half)
            emit(q, base + step_size * jnp.tanh(mixed))

    def grid_of(value):
        return value.reshape(side, side, images, value.shape[-1])

    def to_pad(q, value):
        pad[1 : 1 + side, 1 : 1 + side, :, cut(q)] = grid_of(value)

    def coarse(field, centre, bias):
        mixed = dot(field.astype(jnp.bfloat16), centre) + bias
        return field + 2.0 * step_size * jnp.tanh(mixed)

    def no_wait(h):
        pass

    pad[...] = jnp.zeros_like(pad)
    lanes = 128
    tiles = channels // lanes
    for m in range(images):
        for i in range(side):
            row = img_ref[m, i].astype(jnp.float32)
            for c in range(tiles):
                at = ((m * side + i) * tiles + c) * side
                stage[at : at + side, :] = row[:, c * lanes : (c + 1) * lanes]
    for i in range(side):
        for c in range(tiles):
            for j in range(side):
                at = (i * tiles + c) * side + j
                pad[1 + i, 1 + j, :, c * lanes : (c + 1) * lanes] = stage[
                    pl.ds(at, images, stride=side * tiles * side), :
                ]

    def first_layer(h):
        wait_load(0, h)
        start_load(1, h)

    fine(0, first_layer, to_pad)

    @pl.when(me == 0)
    def _():
        out_ref[0] = pad[1 : 1 + side, 1 : 1 + side]

    pl.semaphore_wait(barrier, 4)

    @pl.when(me >= 2)
    def _():
        centre = wv[0, 4].reshape(channels, channels)
        wsend[0:channels, :] = centre.astype(jnp.float32)
        wsend[channels : channels + 8, :] = jnp.broadcast_to(b_ref[0:1, :], (8, channels))
        send_centre().start()
        wc[core] = centre
        bc[core] = jnp.broadcast_to(b_ref[0:1, :], (8, channels))

    def emit_guess(q, value):
        gsend[q] = value

        @pl.when(has_next)
        def _():
            send_guess(q).start()

    fine(1, lambda h: wait_load(1, h), emit_guess)

    @pl.when(me == 0)
    def _():
        for q in range(2):
            out_ref[1, :, :, :, cut(q)] = grid_of(gsend[q])

    @pl.when(me >= 1)
    def _():
        def arrive(h):
            send_guess(h).wait_recv()
            to_pad(h, shifted[h])

        fine(0, arrive, to_pad)

        @pl.when(me == 1)
        def _():
            out_ref[0] = pad[1 : 1 + side, 1 : 1 + side]

        def emit_end(q, value):
            out_ref[1, :, :, :, cut(q)] = grid_of(value)

        fine(1, no_wait, emit_end)

        @pl.when((me == 1) & has_next_pair)
        def _():
            for g in range(groups):
                for t in range(2):
                    first_coarse(t, g).start()

    @pl.when(me >= 2)
    def _():
        start = jnp.concatenate([shifted[0], shifted[1]], axis=1)
        centre = wv[0, 4].reshape(channels, channels)
        force[...] = out_ref[1] - grid_of(coarse(start, centre, b_ref[0:1, :]))
        send_force().start()
        fo[core] = force[pl.ds(groups * core, groups)]
        send_centre().wait_recv()
        wc[other] = wrecv[0:channels, :].astype(jnp.bfloat16)
        bc[other] = wrecv[channels : channels + 8, :]
        send_force().wait_recv()

        def advance(field, b, g):
            flat = field.reshape(side * images, channels)
            solved = coarse(flat, wc[b], bc[b, 0:1, :])
            return solved.reshape(side, images, channels) + fo[b, g]

        for g in range(groups):
            send_coarse(g).wait_recv()

            @pl.when(core == 1)
            def _():
                send_fin(cin, g).start()

            field = cin[g]
            first = advance(field, 0, g)
            abuf[g] = first

            @pl.when(core == 0)
            def _():
                send_fin(abuf, g).start()

            second = advance(first, 1, g)
            bbuf[g] = second

            @pl.when(has_next_pair)
            def _():
                send_coarse(g).start()

            @pl.when(core == 0)
            def _():
                send_out(bbuf, g).start()

            @pl.when(core == 1)
            def _():
                send_out(abuf, g).start()

            own = groups * core + g
            pad[1 + own, 1 : 1 + side] = jnp.where(core == 0, field, first)
            out_ref[1, own] = jnp.where(core == 0, first, second)

        for g in range(groups):
            send_fin(cin, g).wait_recv()
            pad[1 + groups * other + g, 1 : 1 + side] = peer_fin[g]

        def emit_finished(q, value):
            out_ref[0, :, :, :, cut(q)] = grid_of(value)

        fine(0, no_wait, emit_finished)
        for g in range(groups):
            send_out(abuf, g).wait_recv()
            out_ref[1, groups * other + g] = peer_out[g]

        send_centre().wait_send()
        send_force().wait_send()
        for g in range(groups):
            send_fin(cin, g).wait_send()
            send_out(abuf, g).wait_send()

            @pl.when(has_next_pair)
            def _():
                send_coarse(g).wait_send()

    @pl.when(has_next)
    def _():
        for q in range(2):
            send_guess(q).wait_send()

    @pl.when((me == 1) & has_next_pair)
    def _():
        for g in range(groups):
            for t in range(2):
                first_coarse(t, g).wait_send()


def shards(n, images, weights, biases):
    count, side, _, channels = images.shape
    half = channels // 2
    rows = side * side * count
    groups = side // 2
    piece = (groups, side, count, channels)
    taps = weights.reshape(2, 9, 2, half, channels)
    vmem = pl.BlockSpec(memory_space=pltpu.VMEM)
    f32, bf16 = jnp.float32, jnp.bfloat16
    out = pl.pallas_call(
        functools.partial(kernel, n),
        out_shape=jax.ShapeDtypeStruct((2, side, side, count, channels), f32),
        in_specs=[vmem, pl.BlockSpec(memory_space=pl.ANY), vmem],
        out_specs=vmem,
        scratch_shapes=[
            pltpu.VMEM(taps.shape, bf16),
            pltpu.VMEM((side + 2, side + 2, count, channels), f32),
            pltpu.VMEM((2, rows, 9 * half), bf16),
            pltpu.VMEM((2, rows, half), f32),
            pltpu.VMEM((2, rows, half), f32),
            pltpu.VMEM((rows * channels // 128, 128), f32),
            pltpu.VMEM((side, side, count, channels), f32),
            pltpu.VMEM((channels + 8, channels), f32),
            pltpu.VMEM((channels + 8, channels), f32),
            pltpu.VMEM((2, channels, channels), bf16),
            pltpu.VMEM((2, 8, channels), f32),
            pltpu.VMEM((2,) + piece, f32),
            pltpu.VMEM(piece, f32),
            pltpu.VMEM(piece, f32),
            pltpu.VMEM(piece, f32),
            pltpu.VMEM(piece, f32),
            pltpu.VMEM(piece, f32),
            pltpu.SemaphoreType.DMA((2, 2, 3)),
            pltpu.SemaphoreType.DMA((2, 2)),
            pltpu.SemaphoreType.DMA((2,)),
            pltpu.SemaphoreType.DMA((2,)),
            pltpu.SemaphoreType.DMA((2, groups)),
            pltpu.SemaphoreType.DMA((groups,)),
            pltpu.SemaphoreType.DMA((2, groups)),
            pltpu.SemaphoreType.DMA((2, groups)),
        ],
        compiler_params=pltpu.CompilerParams(
            collective_id=0, has_side_effects=True, vmem_limit_bytes=56 * 2**20
        ),
    )(images, taps, biases)
    return jnp.transpose(out, (0, 3, 1, 2, 4))


def solution(mesh):
    return jax.shard_map(
        functools.partial(shards, mesh.shape["layer"]),
        mesh=mesh,
        in_specs=(P("batch", None, None, None), P("layer", None, None), P("layer", None)),
        out_specs=P("layer", "batch", None, None, None),
        check_vma=False,
    )
```

```python
import functools

import jax
import jax.numpy as jnp
from jax import lax
from jax.experimental import pallas as pl
from jax.experimental.pallas import tpu as pltpu
from jax.sharding import PartitionSpec as P

MESH = pl.DeviceIdType.MESH
step_size = 0.25


def dot(a, b):
    return jnp.dot(a, b, preferred_element_type=jnp.float32)


def kernel(
    n,
    img_hbm,
    w_hbm,
    b_hbm,
    out_ref,
    img_ref,
    b_ref,
    wv,
    pad,
    cols,
    gsend,
    shifted,
    stage,
    force,
    wsend,
    wrecv,
    wc,
    bc,
    fo,
    cin,
    abuf,
    bbuf,
    peer_fin,
    peer_out,
    in_sem,
    w_sem,
    g_sem,
    wx_sem,
    fx_sem,
    cs_sem,
    cr_sem,
    pf_sem,
    po_sem,
):
    me = lax.axis_index("layer")
    right, left = lax.rem(me + 1, n), lax.rem(me + n - 1, n)
    images, side, _, channels = img_ref.shape
    half = channels // 2
    rows = side * side * images
    has_next = me < n - 1
    has_next_pair = me < n - 2
    core = lax.rem(me, 2)
    other = 1 - core
    partner = me + 1 - 2 * core
    ahead, behind = lax.rem(me + 2, n), lax.rem(me + n - 2, n)
    groups = side // 2

    def loads(l, h):
        return [
            pltpu.make_async_copy(
                w_hbm.at[l, 3 * r : 3 * r + 3, h],
                wv.at[l, 3 * r : 3 * r + 3, h],
                w_sem.at[l, h, r],
            )
            for r in range(3)
        ]

    def start_load(l, h):
        for copy in loads(l, h):
            copy.start()

    def wait_load(l, h):
        for copy in loads(l, h):
            copy.wait()

    get_images = pltpu.make_async_copy(img_hbm, img_ref, in_sem.at[0])
    get_biases = pltpu.make_async_copy(b_hbm, b_ref, in_sem.at[1])
    get_images.start()
    get_biases.start()
    start_load(0, 0)
    start_load(0, 1)

    barrier = pltpu.get_barrier_semaphore()
    for neighbour in (left, right, behind, ahead):
        pl.semaphore_signal(
            barrier, inc=1, device_id={"layer": neighbour}, device_id_type=MESH
        )

    def remote(src, dst, send_sem, recv_sem, target):
        return pltpu.make_async_remote_copy(
            src_ref=src,
            dst_ref=dst,
            send_sem=send_sem,
            recv_sem=recv_sem,
            device_id={"layer": target},
            device_id_type=MESH,
        )

    def send_guess(q):
        return remote(gsend.at[q], shifted.at[q], g_sem.at[0, q], g_sem.at[1, q], right)

    def send_centre():
        return remote(wsend, wrecv, wx_sem.at[0], wx_sem.at[1], partner)

    def send_force():
        away = force.at[pl.ds(groups * other, groups)]
        return remote(away, fo.at[core], fx_sem.at[0], fx_sem.at[1], partner)

    def first_coarse(t, g):
        src = out_ref.at[1, groups * t + g]
        return remote(src, cin.at[g], cs_sem.at[t, g], cr_sem.at[g], me + 1 + t)

    def send_coarse(g):
        return remote(bbuf.at[g], cin.at[g], cs_sem.at[0, g], cr_sem.at[g], ahead)

    def send_fin(src, g):
        return remote(src.at[g], peer_fin.at[g], pf_sem.at[0, g], pf_sem.at[1, g], partner)

    def send_out(src, g):
        return remote(src.at[g], peer_out.at[g], po_sem.at[0, g], po_sem.at[1, g], partner)

    def cut(h):
        return slice(h * half, (h + 1) * half)

    def build(h):
        for tap in range(9):
            dy, dx = tap // 3, tap % 3
            piece = pad[dy : dy + side, dx : dx + side, :, cut(h)]
            cols[h, :, tap * half : (tap + 1) * half] = piece.reshape(rows, half).astype(
                jnp.bfloat16
            )

    def weight(l, h, q):
        return wv[l, :, h, :, cut(q)].reshape(9 * half, half)

    def fine(l, before, emit):
        before(0)
        build(0)
        parts = [dot(cols[0], weight(l, 0, q)) for q in range(2)]
        before(1)
        build(1)
        for q in range(2):
            mixed = parts[q] + dot(cols[1], weight(l, 1, q)) + b_ref[l : l + 1, cut(q)]
            base = pad[1 : 1 + side, 1 : 1 + side, :, cut(q)].reshape(rows, half)
            emit(q, base + step_size * jnp.tanh(mixed))

    def grid_of(value):
        return value.reshape(side, side, images, value.shape[-1])

    def to_pad(q, value):
        pad[1 : 1 + side, 1 : 1 + side, :, cut(q)] = grid_of(value)

    def coarse(field, centre, bias):
        mixed = dot(field.astype(jnp.bfloat16), centre) + bias
        return field + 2.0 * step_size * jnp.tanh(mixed)

    def no_wait(h):
        pass

    pad[...] = jnp.zeros_like(pad)
    get_images.wait()
    get_biases.wait()
    lanes = 128
    tiles = channels // lanes
    for m in range(images):
        for i in range(side):
            row = img_ref[m, i].astype(jnp.float32)
            for c in range(tiles):
                at = ((m * side + i) * tiles + c) * side
                stage[at : at + side, :] = row[:, c * lanes : (c + 1) * lanes]
    for i in range(side):
        for c in range(tiles):
            for j in range(side):
                at = (i * tiles + c) * side + j
                pad[1 + i, 1 + j, :, c * lanes : (c + 1) * lanes] = stage[
                    pl.ds(at, images, stride=side * tiles * side), :
                ]

    def first_layer(h):
        wait_load(0, h)
        start_load(1, h)

    fine(0, first_layer, to_pad)

    @pl.when(me == 0)
    def _():
        out_ref[0] = pad[1 : 1 + side, 1 : 1 + side]

    pl.semaphore_wait(barrier, 4)

    @pl.when(me >= 2)
    def _():
        centre = wv[0, 4].reshape(channels, channels)
        wsend[0:channels, :] = centre.astype(jnp.float32)
        wsend[channels : channels + 8, :] = jnp.broadcast_to(b_ref[0:1, :], (8, channels))
        send_centre().start()
        wc[core] = centre
        bc[core] = jnp.broadcast_to(b_ref[0:1, :], (8, channels))

    def emit_guess(q, value):
        gsend[q] = value

        @pl.when(has_next)
        def _():
            send_guess(q).start()

    fine(1, lambda h: wait_load(1, h), emit_guess)

    @pl.when(me == 0)
    def _():
        for q in range(2):
            out_ref[1, :, :, :, cut(q)] = grid_of(gsend[q])

    @pl.when(me >= 1)
    def _():
        def arrive(h):
            send_guess(h).wait_recv()
            to_pad(h, shifted[h])

        fine(0, arrive, to_pad)

        @pl.when(me == 1)
        def _():
            out_ref[0] = pad[1 : 1 + side, 1 : 1 + side]

        def emit_end(q, value):
            out_ref[1, :, :, :, cut(q)] = grid_of(value)

        fine(1, no_wait, emit_end)

        @pl.when((me == 1) & has_next_pair)
        def _():
            for g in range(groups):
                for t in range(2):
                    first_coarse(t, g).start()

    @pl.when(me >= 2)
    def _():
        start = jnp.concatenate([shifted[0], shifted[1]], axis=1)
        centre = wv[0, 4].reshape(channels, channels)
        force[...] = out_ref[1] - grid_of(coarse(start, centre, b_ref[0:1, :]))
        send_force().start()
        fo[core] = force[pl.ds(groups * core, groups)]
        send_centre().wait_recv()
        wc[other] = wrecv[0:channels, :].astype(jnp.bfloat16)
        bc[other] = wrecv[channels : channels + 8, :]
        send_force().wait_recv()

        def advance(field, b, g):
            flat = field.reshape(side * images, channels)
            solved = coarse(flat, wc[b], bc[b, 0:1, :])
            return solved.reshape(side, images, channels) + fo[b, g]

        for g in range(groups):
            send_coarse(g).wait_recv()

            @pl.when(core == 1)
            def _():
                send_fin(cin, g).start()

            field = cin[g]
            first = advance(field, 0, g)
            abuf[g] = first

            @pl.when(core == 0)
            def _():
                send_fin(abuf, g).start()

            second = advance(first, 1, g)
            bbuf[g] = second

            @pl.when(has_next_pair)
            def _():
                send_coarse(g).start()

            @pl.when(core == 0)
            def _():
                send_out(bbuf, g).start()

            @pl.when(core == 1)
            def _():
                send_out(abuf, g).start()

            own = groups * core + g
            pad[1 + own, 1 : 1 + side] = jnp.where(core == 0, field, first)
            out_ref[1, own] = jnp.where(core == 0, first, second)

        for g in range(groups):
            send_fin(cin, g).wait_recv()
            pad[1 + groups * other + g, 1 : 1 + side] = peer_fin[g]

        def emit_finished(q, value):
            out_ref[0, :, :, :, cut(q)] = grid_of(value)

        fine(0, no_wait, emit_finished)
        for g in range(groups):
            send_out(abuf, g).wait_recv()
            out_ref[1, groups * other + g] = peer_out[g]

        send_centre().wait_send()
        send_force().wait_send()
        for g in range(groups):
            send_fin(cin, g).wait_send()
            send_out(abuf, g).wait_send()

            @pl.when(has_next_pair)
            def _():
                send_coarse(g).wait_send()

    @pl.when(has_next)
    def _():
        for q in range(2):
            send_guess(q).wait_send()

    @pl.when((me == 1) & has_next_pair)
    def _():
        for g in range(groups):
            for t in range(2):
                first_coarse(t, g).wait_send()


def shards(n, images, weights, biases):
    count, side, _, channels = images.shape
    half = channels // 2
    rows = side * side * count
    groups = side // 2
    piece = (groups, side, count, channels)
    taps = weights.reshape(2, 9, 2, half, channels)
    vmem = pl.BlockSpec(memory_space=pltpu.VMEM)
    hbm = pl.BlockSpec(memory_space=pl.ANY)
    f32, bf16 = jnp.float32, jnp.bfloat16
    out = pl.pallas_call(
        functools.partial(kernel, n),
        out_shape=pltpu.VMEM((2, side, side, count, channels), f32),
        in_specs=[hbm, hbm, hbm],
        out_specs=vmem,
        scratch_shapes=[
            pltpu.VMEM(images.shape, bf16),
            pltpu.VMEM(biases.shape, f32),
            pltpu.VMEM(taps.shape, bf16),
            pltpu.VMEM((side + 2, side + 2, count, channels), f32),
            pltpu.VMEM((2, rows, 9 * half), bf16),
            pltpu.VMEM((2, rows, half), f32),
            pltpu.VMEM((2, rows, half), f32),
            pltpu.VMEM((rows * channels // 128, 128), f32),
            pltpu.VMEM((side, side, count, channels), f32),
            pltpu.VMEM((channels + 8, channels), f32),
            pltpu.VMEM((channels + 8, channels), f32),
            pltpu.VMEM((2, channels, channels), bf16),
            pltpu.VMEM((2, 8, channels), f32),
            pltpu.VMEM((2,) + piece, f32),
            pltpu.VMEM(piece, f32),
            pltpu.VMEM(piece, f32),
            pltpu.VMEM(piece, f32),
            pltpu.VMEM(piece, f32),
            pltpu.VMEM(piece, f32),
            pltpu.SemaphoreType.DMA((2,)),
            pltpu.SemaphoreType.DMA((2, 2, 3)),
            pltpu.SemaphoreType.DMA((2, 2)),
            pltpu.SemaphoreType.DMA((2,)),
            pltpu.SemaphoreType.DMA((2,)),
            pltpu.SemaphoreType.DMA((2, groups)),
            pltpu.SemaphoreType.DMA((groups,)),
            pltpu.SemaphoreType.DMA((2, groups)),
            pltpu.SemaphoreType.DMA((2, groups)),
        ],
        compiler_params=pltpu.CompilerParams(
            collective_id=0, has_side_effects=True, vmem_limit_bytes=56 * 2**20
        ),
    )(images, taps, biases)
    return jnp.transpose(out, (0, 3, 1, 2, 4))


def solution(mesh):
    return jax.shard_map(
        functools.partial(shards, mesh.shape["layer"]),
        mesh=mesh,
        in_specs=(P("batch", None, None, None), P("layer", None, None), P("layer", None)),
        out_specs=P("layer", "batch", None, None, None),
        check_vma=False,
    )
```

```python
import functools

import jax
import jax.numpy as jnp
from jax import lax
from jax.experimental import pallas as pl
from jax.experimental.pallas import tpu as pltpu
from jax.sharding import PartitionSpec as P

MESH = pl.DeviceIdType.MESH
step_size = 0.25


def dot(a, b):
    return jnp.dot(a, b, preferred_element_type=jnp.float32)


def kernel(
    n,
    img_hbm,
    w_hbm,
    b_hbm,
    out_ref,
    img_ref,
    b_ref,
    wv,
    pad,
    cols,
    gsend,
    shifted,
    stage,
    force,
    wsend,
    wrecv,
    wc,
    bc,
    fo,
    cin,
    abuf,
    bbuf,
    peer_fin,
    peer_out,
    in_sem,
    w_sem,
    g_sem,
    wx_sem,
    fx_sem,
    cs_sem,
    cr_sem,
    pf_sem,
    po_sem,
):
    me = lax.axis_index("layer")
    right = lax.rem(me + 1, n)
    images, side, _, channels = img_ref.shape
    half = channels // 2
    rows = side * side * images
    has_next = me < n - 1
    has_next_pair = me < n - 2
    core = lax.rem(me, 2)
    other = 1 - core
    partner = me + 1 - 2 * core
    runs = (me >= 2) & (core == jnp.where(has_next_pair, 0, 1))
    helps = (me >= 2) & (core == jnp.where(has_next_pair, 1, 0))
    runner_ahead = jnp.where(me == n - 4, n - 1, lax.rem(me + 2, n))
    groups = side

    def loads(l, h):
        return [
            pltpu.make_async_copy(
                w_hbm.at[l, 3 * r : 3 * r + 3, h],
                wv.at[l, 3 * r : 3 * r + 3, h],
                w_sem.at[l, h, r],
            )
            for r in range(3)
        ]

    def start_load(l, h):
        for copy in loads(l, h):
            copy.start()

    def wait_load(l, h):
        for copy in loads(l, h):
            copy.wait()

    get_images = pltpu.make_async_copy(img_hbm, img_ref, in_sem.at[0])
    get_biases = pltpu.make_async_copy(b_hbm, b_ref, in_sem.at[1])
    get_images.start()
    get_biases.start()
    start_load(0, 0)
    start_load(0, 1)

    barrier = pltpu.get_barrier_semaphore()
    for distance in (1, 2, 3, n - 3, n - 2, n - 1):
        neighbour = lax.rem(me + distance, n)
        pl.semaphore_signal(
            barrier, inc=1, device_id={"layer": neighbour}, device_id_type=MESH
        )

    def remote(src, dst, send_sem, recv_sem, target):
        return pltpu.make_async_remote_copy(
            src_ref=src,
            dst_ref=dst,
            send_sem=send_sem,
            recv_sem=recv_sem,
            device_id={"layer": target},
            device_id_type=MESH,
        )

    def send_guess(q):
        return remote(gsend.at[q], shifted.at[q], g_sem.at[0, q], g_sem.at[1, q], right)

    def send_centre():
        return remote(wsend, wrecv, wx_sem.at[0], wx_sem.at[1], partner)

    def send_force():
        return remote(force, fo.at[core], fx_sem.at[0], fx_sem.at[1], partner)

    def first_coarse(g):
        src = out_ref.at[1, g]
        return remote(src, cin.at[g], cs_sem.at[g], cr_sem.at[g], 2 if n > 4 else n - 1)

    def send_coarse(g):
        return remote(bbuf.at[g], cin.at[g], cs_sem.at[g], cr_sem.at[g], runner_ahead)

    def send_fin(src, g):
        return remote(src.at[g], peer_fin.at[g], pf_sem.at[0, g], pf_sem.at[1, g], partner)

    def send_out(src, g):
        return remote(src.at[g], peer_out.at[g], po_sem.at[0, g], po_sem.at[1, g], partner)

    def cut(h):
        return slice(h * half, (h + 1) * half)

    def build(h):
        for tap in range(9):
            dy, dx = tap // 3, tap % 3
            piece = pad[dy : dy + side, dx : dx + side, :, cut(h)]
            cols[h, :, tap * half : (tap + 1) * half] = piece.reshape(rows, half).astype(
                jnp.bfloat16
            )

    def weight(l, h, q):
        return wv[l, :, h, :, cut(q)].reshape(9 * half, half)

    def fine(l, before, emit):
        before(0)
        build(0)
        parts = [dot(cols[0], weight(l, 0, q)) for q in range(2)]
        before(1)
        build(1)
        for q in range(2):
            mixed = parts[q] + dot(cols[1], weight(l, 1, q)) + b_ref[l : l + 1, cut(q)]
            base = pad[1 : 1 + side, 1 : 1 + side, :, cut(q)].reshape(rows, half)
            emit(q, base + step_size * jnp.tanh(mixed))

    def grid_of(value):
        return value.reshape(side, side, images, value.shape[-1])

    def to_pad(q, value):
        pad[1 : 1 + side, 1 : 1 + side, :, cut(q)] = grid_of(value)

    def coarse(field, centre, bias):
        mixed = dot(field.astype(jnp.bfloat16), centre) + bias
        return field + 2.0 * step_size * jnp.tanh(mixed)

    def no_wait(h):
        pass

    pad[...] = jnp.zeros_like(pad)
    get_images.wait()
    get_biases.wait()
    lanes = 128
    tiles = channels // lanes
    for m in range(images):
        for i in range(side):
            row = img_ref[m, i].astype(jnp.float32)
            for c in range(tiles):
                at = ((m * side + i) * tiles + c) * side
                stage[at : at + side, :] = row[:, c * lanes : (c + 1) * lanes]
    for i in range(side):
        for c in range(tiles):
            for j in range(side):
                at = (i * tiles + c) * side + j
                pad[1 + i, 1 + j, :, c * lanes : (c + 1) * lanes] = stage[
                    pl.ds(at, images, stride=side * tiles * side), :
                ]

    def first_layer(h):
        wait_load(0, h)
        start_load(1, h)

    fine(0, first_layer, to_pad)

    @pl.when(me == 0)
    def _():
        out_ref[0] = pad[1 : 1 + side, 1 : 1 + side]

    pl.semaphore_wait(barrier, 6)

    @pl.when(helps)
    def _():
        centre = wv[0, 4].reshape(channels, channels)
        wsend[0:channels, :] = centre.astype(jnp.float32)
        wsend[channels : channels + 8, :] = jnp.broadcast_to(b_ref[0:1, :], (8, channels))
        send_centre().start()

    @pl.when(runs)
    def _():
        wc[core] = wv[0, 4].reshape(channels, channels)
        bc[core] = jnp.broadcast_to(b_ref[0:1, :], (8, channels))

    def emit_guess(q, value):
        gsend[q] = value

        @pl.when(has_next)
        def _():
            send_guess(q).start()

    fine(1, lambda h: wait_load(1, h), emit_guess)

    @pl.when(me == 0)
    def _():
        for q in range(2):
            out_ref[1, :, :, :, cut(q)] = grid_of(gsend[q])

    @pl.when(me >= 1)
    def _():
        def arrive(h):
            send_guess(h).wait_recv()
            to_pad(h, shifted[h])

        fine(0, arrive, to_pad)

        @pl.when(me == 1)
        def _():
            out_ref[0] = pad[1 : 1 + side, 1 : 1 + side]

        def emit_end(q, value):
            out_ref[1, :, :, :, cut(q)] = grid_of(value)

        fine(1, no_wait, emit_end)

        @pl.when((me == 1) & has_next_pair)
        def _():
            for g in range(groups):
                first_coarse(g).start()

    def own_forcing():
        start = jnp.concatenate([shifted[0], shifted[1]], axis=1)
        centre = wv[0, 4].reshape(channels, channels)
        return out_ref[1] - grid_of(coarse(start, centre, b_ref[0:1, :]))

    def emit_finished(q, value):
        out_ref[0, :, :, :, cut(q)] = grid_of(value)

    @pl.when(runs)
    def _():
        fo[core] = own_forcing()
        send_centre().wait_recv()
        wc[other] = wrecv[0:channels, :].astype(jnp.bfloat16)
        bc[other] = wrecv[channels : channels + 8, :]
        send_force().wait_recv()

        def advance(field, b, g):
            flat = field.reshape(side * images, channels)
            solved = coarse(flat, wc[b], bc[b, 0:1, :])
            return solved.reshape(side, images, channels) + fo[b, g]

        for g in range(groups):
            send_coarse(g).wait_recv()

            @pl.when(core == 1)
            def _():
                send_fin(cin, g).start()

            field = cin[g]
            first = advance(field, 0, g)
            abuf[g] = first
            second = advance(first, 1, g)
            bbuf[g] = second

            @pl.when(has_next_pair)
            def _():
                send_coarse(g).start()
                send_fin(abuf, g).start()
                send_out(bbuf, g).start()

            @pl.when(core == 1)
            def _():
                send_out(abuf, g).start()

            pad[1 + g, 1 : 1 + side] = jnp.where(core == 0, field, first)
            out_ref[1, g] = jnp.where(core == 0, first, second)

        fine(0, no_wait, emit_finished)
        for g in range(groups):
            send_fin(cin, g).wait_send()
            send_out(abuf, g).wait_send()

            @pl.when(has_next_pair)
            def _():
                send_coarse(g).wait_send()

    @pl.when(helps)
    def _():
        force[...] = own_forcing()
        send_force().start()
        for g in range(groups):
            send_fin(cin, g).wait_recv()
            pad[1 + g, 1 : 1 + side] = peer_fin[g]
        fine(0, no_wait, emit_finished)
        for g in range(groups):
            send_out(abuf, g).wait_recv()
            out_ref[1, g] = peer_out[g]
        send_centre().wait_send()
        send_force().wait_send()

    @pl.when(has_next)
    def _():
        for q in range(2):
            send_guess(q).wait_send()

    @pl.when((me == 1) & has_next_pair)
    def _():
        for g in range(groups):
            first_coarse(g).wait_send()


def shards(n, images, weights, biases):
    count, side, _, channels = images.shape
    half = channels // 2
    rows = side * side * count
    groups = side
    piece = (groups, side, count, channels)
    taps = weights.reshape(2, 9, 2, half, channels)
    vmem = pl.BlockSpec(memory_space=pltpu.VMEM)
    hbm = pl.BlockSpec(memory_space=pl.ANY)
    f32, bf16 = jnp.float32, jnp.bfloat16
    out = pl.pallas_call(
        functools.partial(kernel, n),
        out_shape=pltpu.VMEM((2, side, side, count, channels), f32),
        in_specs=[hbm, hbm, hbm],
        out_specs=vmem,
        scratch_shapes=[
            pltpu.VMEM(images.shape, bf16),
            pltpu.VMEM(biases.shape, f32),
            pltpu.VMEM(taps.shape, bf16),
            pltpu.VMEM((side + 2, side + 2, count, channels), f32),
            pltpu.VMEM((2, rows, 9 * half), bf16),
            pltpu.VMEM((2, rows, half), f32),
            pltpu.VMEM((2, rows, half), f32),
            pltpu.VMEM((rows * channels // 128, 128), f32),
            pltpu.VMEM((side, side, count, channels), f32),
            pltpu.VMEM((channels + 8, channels), f32),
            pltpu.VMEM((channels + 8, channels), f32),
            pltpu.VMEM((2, channels, channels), bf16),
            pltpu.VMEM((2, 8, channels), f32),
            pltpu.VMEM((2,) + piece, f32),
            pltpu.VMEM(piece, f32),
            pltpu.VMEM(piece, f32),
            pltpu.VMEM(piece, f32),
            pltpu.VMEM(piece, f32),
            pltpu.VMEM(piece, f32),
            pltpu.SemaphoreType.DMA((2,)),
            pltpu.SemaphoreType.DMA((2, 2, 3)),
            pltpu.SemaphoreType.DMA((2, 2)),
            pltpu.SemaphoreType.DMA((2,)),
            pltpu.SemaphoreType.DMA((2,)),
            pltpu.SemaphoreType.DMA((groups,)),
            pltpu.SemaphoreType.DMA((groups,)),
            pltpu.SemaphoreType.DMA((2, groups)),
            pltpu.SemaphoreType.DMA((2, groups)),
        ],
        compiler_params=pltpu.CompilerParams(
            collective_id=0, has_side_effects=True, vmem_limit_bytes=56 * 2**20
        ),
    )(images, taps, biases)
    return jnp.transpose(out, (0, 3, 1, 2, 4))


def solution(mesh):
    return jax.shard_map(
        functools.partial(shards, mesh.shape["layer"]),
        mesh=mesh,
        in_specs=(P("batch", None, None, None), P("layer", None, None), P("layer", None)),
        out_specs=P("layer", "batch", None, None, None),
        check_vma=False,
    )
```

```python
import functools

import jax
import jax.numpy as jnp
from jax import lax
from jax.experimental import pallas as pl
from jax.experimental.pallas import tpu as pltpu
from jax.sharding import PartitionSpec as P

MESH = pl.DeviceIdType.MESH
step_size = 0.25


def dot(a, b):
    return jnp.dot(a, b, preferred_element_type=jnp.float32)


def kernel(
    n,
    img_hbm,
    w_hbm,
    b_hbm,
    out_ref,
    img_ref,
    b_ref,
    wv,
    pad,
    cols,
    gsend,
    shifted,
    stage,
    centre_dot,
    force,
    wsend,
    wrecv,
    wc,
    bc,
    fo,
    cin,
    abuf,
    bbuf,
    peer_fin,
    peer_out,
    in_sem,
    w_sem,
    g_sem,
    wx_sem,
    fx_sem,
    cs_sem,
    cr_sem,
    pf_sem,
    po_sem,
):
    me = lax.axis_index("layer")
    right = lax.rem(me + 1, n)
    images, side, _, channels = img_ref.shape
    half = channels // 2
    rows = side * side * images
    has_next = me < n - 1
    has_next_pair = me < n - 2
    core = lax.rem(me, 2)
    other = 1 - core
    partner = me + 1 - 2 * core
    runs = (me >= 2) & (core == jnp.where(has_next_pair, 0, 1))
    helps = (me >= 2) & (core == jnp.where(has_next_pair, 1, 0))
    runner_ahead = jnp.where(me == n - 4, n - 1, lax.rem(me + 2, n))
    groups = side

    def loads(l, h):
        return [
            pltpu.make_async_copy(
                w_hbm.at[l, 3 * r : 3 * r + 3, h],
                wv.at[l, 3 * r : 3 * r + 3, h],
                w_sem.at[l, h, r],
            )
            for r in range(3)
        ]

    def start_load(l, h):
        for copy in loads(l, h):
            copy.start()

    def wait_load(l, h):
        for copy in loads(l, h):
            copy.wait()

    get_images = pltpu.make_async_copy(img_hbm, img_ref, in_sem.at[0])
    get_biases = pltpu.make_async_copy(b_hbm, b_ref, in_sem.at[1])
    get_images.start()
    get_biases.start()
    start_load(0, 0)
    start_load(0, 1)

    barrier = pltpu.get_barrier_semaphore()
    for distance in (1, 2, 3, n - 3, n - 2, n - 1):
        neighbour = lax.rem(me + distance, n)
        pl.semaphore_signal(
            barrier, inc=1, device_id={"layer": neighbour}, device_id_type=MESH
        )

    def remote(src, dst, send_sem, recv_sem, target):
        return pltpu.make_async_remote_copy(
            src_ref=src,
            dst_ref=dst,
            send_sem=send_sem,
            recv_sem=recv_sem,
            device_id={"layer": target},
            device_id_type=MESH,
        )

    def send_guess(q):
        return remote(gsend.at[q], shifted.at[q], g_sem.at[0, q], g_sem.at[1, q], right)

    def send_centre():
        return remote(wsend, wrecv, wx_sem.at[0], wx_sem.at[1], partner)

    def send_force():
        return remote(force, fo.at[core], fx_sem.at[0], fx_sem.at[1], partner)

    def first_coarse(g):
        src = out_ref.at[1, g]
        return remote(src, cin.at[g], cs_sem.at[g], cr_sem.at[g], 2 if n > 4 else n - 1)

    def send_coarse(g):
        return remote(bbuf.at[g], cin.at[g], cs_sem.at[g], cr_sem.at[g], runner_ahead)

    def send_fin(src, g):
        return remote(src.at[g], peer_fin.at[g], pf_sem.at[0, g], pf_sem.at[1, g], partner)

    def send_out(src, g):
        return remote(src.at[g], peer_out.at[g], po_sem.at[0, g], po_sem.at[1, g], partner)

    def cut(h):
        return slice(h * half, (h + 1) * half)

    band = side * images

    def build(h):
        for dx in range(3):
            piece = pad[1 : 1 + side, dx : dx + side, :, cut(h)]
            cols[h, band : band + rows, dx * half : (dx + 1) * half] = piece.reshape(
                rows, half
            ).astype(jnp.bfloat16)

    def taps_of(l, h, q):
        total = None
        for dy in range(3):
            window = cols[h, dy * band : dy * band + rows, :]
            block = wv[l, 3 * dy : 3 * dy + 3, h, :, cut(q)].reshape(3 * half, half)
            part = dot(window, block)
            total = part if total is None else total + part
        return total

    def fine(l, before, emit):
        before(0)
        build(0)
        parts = [taps_of(l, 0, q) for q in range(2)]
        before(1)
        build(1)
        for q in range(2):
            mixed = parts[q] + taps_of(l, 1, q) + b_ref[l : l + 1, cut(q)]
            base = pad[1 : 1 + side, 1 : 1 + side, :, cut(q)].reshape(rows, half)
            emit(q, base + step_size * jnp.tanh(mixed))

    def grid_of(value):
        return value.reshape(side, side, images, value.shape[-1])

    def to_pad(q, value):
        pad[1 : 1 + side, 1 : 1 + side, :, cut(q)] = grid_of(value)

    def coarse(field, centre, bias):
        mixed = dot(field.astype(jnp.bfloat16), centre) + bias
        return field + 2.0 * step_size * jnp.tanh(mixed)

    def no_wait(h):
        pass

    pad[...] = jnp.zeros_like(pad)
    for h in range(2):
        cols[h, 0:band, :] = jnp.zeros((band, 3 * half), jnp.bfloat16)
        cols[h, band + rows :, :] = jnp.zeros((band, 3 * half), jnp.bfloat16)
    get_images.wait()
    get_biases.wait()
    lanes = 128
    tiles = channels // lanes
    for m in range(images):
        for i in range(side):
            row = img_ref[m, i].astype(jnp.float32)
            for c in range(tiles):
                at = ((m * side + i) * tiles + c) * side
                stage[at : at + side, :] = row[:, c * lanes : (c + 1) * lanes]
    for i in range(side):
        for c in range(tiles):
            for j in range(side):
                at = (i * tiles + c) * side + j
                pad[1 + i, 1 + j, :, c * lanes : (c + 1) * lanes] = stage[
                    pl.ds(at, images, stride=side * tiles * side), :
                ]

    def first_layer(h):
        wait_load(0, h)
        start_load(1, h)

    fine(0, first_layer, to_pad)

    @pl.when(me == 0)
    def _():
        out_ref[0] = pad[1 : 1 + side, 1 : 1 + side]

    pl.semaphore_wait(barrier, 6)

    @pl.when(helps)
    def _():
        centre = wv[0, 4].reshape(channels, channels)
        wsend[0:channels, :] = centre.astype(jnp.float32)
        wsend[channels : channels + 8, :] = jnp.broadcast_to(b_ref[0:1, :], (8, channels))
        send_centre().start()

    @pl.when(runs)
    def _():
        wc[core] = wv[0, 4].reshape(channels, channels)
        bc[core] = jnp.broadcast_to(b_ref[0:1, :], (8, channels))

    def emit_guess(q, value):
        gsend[q] = value

        @pl.when(has_next)
        def _():
            send_guess(q).start()

    fine(1, lambda h: wait_load(1, h), emit_guess)

    @pl.when(me == 0)
    def _():
        for q in range(2):
            out_ref[1, :, :, :, cut(q)] = grid_of(gsend[q])

    @pl.when(me >= 1)
    def _():
        def arrive(h):
            if h == 0:

                @pl.when(runs)
                def _():
                    send_centre().wait_recv()
                    wc[other] = wrecv[0:channels, :].astype(jnp.bfloat16)
                    bc[other] = wrecv[channels : channels + 8, :]

            else:

                @pl.when(me >= 2)
                def _():
                    centre_dot[...] = dot(shifted[0].astype(jnp.bfloat16), wv[0, 4, 0])

            send_guess(h).wait_recv()
            to_pad(h, shifted[h])

        fine(0, arrive, to_pad)

        @pl.when(me == 1)
        def _():
            out_ref[0] = pad[1 : 1 + side, 1 : 1 + side]

        def emit_end(q, value):
            out_ref[1, :, :, :, cut(q)] = grid_of(value)

        fine(1, no_wait, emit_end)

        @pl.when((me == 1) & has_next_pair)
        def _():
            for g in range(groups):
                first_coarse(g).start()

    def own_forcing():
        start = jnp.concatenate([shifted[0], shifted[1]], axis=1)
        rest = dot(shifted[1].astype(jnp.bfloat16), wv[0, 4, 1])
        mixed = centre_dot[...] + rest + b_ref[0:1, :]
        return out_ref[1] - grid_of(start + 2.0 * step_size * jnp.tanh(mixed))

    def emit_finished(q, value):
        out_ref[0, :, :, :, cut(q)] = grid_of(value)

    @pl.when(runs)
    def _():
        fo[core] = own_forcing()
        send_force().wait_recv()

        def advance(field, b, g):
            flat = field.reshape(side * images, channels)
            solved = coarse(flat, wc[b], bc[b, 0:1, :])
            return solved.reshape(side, images, channels) + fo[b, g]

        for g in range(groups):
            send_coarse(g).wait_recv()

            @pl.when(core == 1)
            def _():
                send_fin(cin, g).start()

            field = cin[g]
            first = advance(field, 0, g)
            abuf[g] = first
            second = advance(first, 1, g)
            bbuf[g] = second

            @pl.when(has_next_pair)
            def _():
                send_coarse(g).start()
                send_fin(abuf, g).start()
                send_out(bbuf, g).start()

            @pl.when(core == 1)
            def _():
                send_out(abuf, g).start()

            pad[1 + g, 1 : 1 + side] = jnp.where(core == 0, field, first)
            out_ref[1, g] = jnp.where(core == 0, first, second)

        fine(0, no_wait, emit_finished)
        for g in range(groups):
            send_fin(cin, g).wait_send()
            send_out(abuf, g).wait_send()

            @pl.when(has_next_pair)
            def _():
                send_coarse(g).wait_send()

    @pl.when(helps)
    def _():
        force[...] = own_forcing()
        send_force().start()
        for g in range(groups):
            send_fin(cin, g).wait_recv()
            pad[1 + g, 1 : 1 + side] = peer_fin[g]
        fine(0, no_wait, emit_finished)
        for g in range(groups):
            send_out(abuf, g).wait_recv()
            out_ref[1, g] = peer_out[g]
        send_centre().wait_send()
        send_force().wait_send()

    @pl.when(has_next)
    def _():
        for q in range(2):
            send_guess(q).wait_send()

    @pl.when((me == 1) & has_next_pair)
    def _():
        for g in range(groups):
            first_coarse(g).wait_send()


def shards(n, images, weights, biases):
    count, side, _, channels = images.shape
    half = channels // 2
    rows = side * side * count
    groups = side
    piece = (groups, side, count, channels)
    taps = weights.reshape(2, 9, 2, half, channels)
    vmem = pl.BlockSpec(memory_space=pltpu.VMEM)
    hbm = pl.BlockSpec(memory_space=pl.ANY)
    f32, bf16 = jnp.float32, jnp.bfloat16
    out = pl.pallas_call(
        functools.partial(kernel, n),
        out_shape=pltpu.VMEM((2, side, side, count, channels), f32),
        in_specs=[hbm, hbm, hbm],
        out_specs=vmem,
        scratch_shapes=[
            pltpu.VMEM(images.shape, bf16),
            pltpu.VMEM(biases.shape, f32),
            pltpu.VMEM(taps.shape, bf16),
            pltpu.VMEM((side + 2, side + 2, count, channels), f32),
            pltpu.VMEM((2, rows + 2 * side * count, 3 * half), bf16),
            pltpu.VMEM((2, rows, half), f32),
            pltpu.VMEM((2, rows, half), f32),
            pltpu.VMEM((rows * channels // 128, 128), f32),
            pltpu.VMEM((rows, channels), f32),
            pltpu.VMEM((side, side, count, channels), f32),
            pltpu.VMEM((channels + 8, channels), f32),
            pltpu.VMEM((channels + 8, channels), f32),
            pltpu.VMEM((2, channels, channels), bf16),
            pltpu.VMEM((2, 8, channels), f32),
            pltpu.VMEM((2,) + piece, f32),
            pltpu.VMEM(piece, f32),
            pltpu.VMEM(piece, f32),
            pltpu.VMEM(piece, f32),
            pltpu.VMEM(piece, f32),
            pltpu.VMEM(piece, f32),
            pltpu.SemaphoreType.DMA((2,)),
            pltpu.SemaphoreType.DMA((2, 2, 3)),
            pltpu.SemaphoreType.DMA((2, 2)),
            pltpu.SemaphoreType.DMA((2,)),
            pltpu.SemaphoreType.DMA((2,)),
            pltpu.SemaphoreType.DMA((groups,)),
            pltpu.SemaphoreType.DMA((groups,)),
            pltpu.SemaphoreType.DMA((2, groups)),
            pltpu.SemaphoreType.DMA((2, groups)),
        ],
        compiler_params=pltpu.CompilerParams(
            collective_id=0, has_side_effects=True, vmem_limit_bytes=56 * 2**20
        ),
    )(images, taps, biases)
    return jnp.transpose(out, (0, 3, 1, 2, 4))


def solution(mesh):
    return jax.shard_map(
        functools.partial(shards, mesh.shape["layer"]),
        mesh=mesh,
        in_specs=(P("batch", None, None, None), P("layer", None, None), P("layer", None)),
        out_specs=P("layer", "batch", None, None, None),
        check_vma=False,
    )
```

```python
import functools

import jax
import jax.numpy as jnp
from jax import lax
from jax.experimental import pallas as pl
from jax.experimental.pallas import tpu as pltpu
from jax.sharding import PartitionSpec as P

MESH = pl.DeviceIdType.MESH
step_size = 0.25


def dot(a, b):
    return jnp.dot(a, b, preferred_element_type=jnp.float32)


def kernel(
    n,
    img_hbm,
    w_hbm,
    b_hbm,
    out_ref,
    img_ref,
    b_ref,
    wv,
    pad,
    cols,
    gsend,
    shifted,
    stage,
    centre_dot,
    force,
    wsend,
    wrecv,
    wc,
    bc,
    fo,
    cin,
    abuf,
    bbuf,
    peer_fin,
    peer_out,
    guess_over,
    rows_over,
    go_sem,
    ro_sem,
    in_sem,
    w_sem,
    g_sem,
    wx_sem,
    fx_sem,
    cs_sem,
    cr_sem,
    pf_sem,
    po_sem,
):
    me = lax.axis_index("layer")
    right = lax.rem(me + 1, n)
    images, side, _, channels = img_ref.shape
    half = channels // 2
    rows = side * side * images
    has_next = me < n - 1
    has_next_pair = me < n - 2
    core = lax.rem(me, 2)
    other = 1 - core
    partner = me + 1 - 2 * core
    runs = (me >= 2) & (core == jnp.where(has_next_pair, 0, 1))
    helps = (me >= 2) & (core == jnp.where(has_next_pair, 1, 0))
    runner_ahead = jnp.where(me == n - 4, n - 1, lax.rem(me + 2, n))
    groups = side

    def loads(l, h):
        return [
            pltpu.make_async_copy(
                w_hbm.at[l, 3 * r : 3 * r + 3, h],
                wv.at[l, 3 * r : 3 * r + 3, h],
                w_sem.at[l, h, r],
            )
            for r in range(3)
        ]

    def start_load(l, h):
        for copy in loads(l, h):
            copy.start()

    def wait_load(l, h):
        for copy in loads(l, h):
            copy.wait()

    get_images = pltpu.make_async_copy(img_hbm, img_ref, in_sem.at[0])
    get_biases = pltpu.make_async_copy(b_hbm, b_ref, in_sem.at[1])
    get_images.start()
    get_biases.start()
    start_load(0, 0)
    start_load(0, 1)

    barrier = pltpu.get_barrier_semaphore()
    forwards = n == 8
    distances = range(1, n) if forwards else (1, 2, 3, n - 3, n - 2, n - 1)
    for distance in distances:
        neighbour = lax.rem(me + distance, n)
        pl.semaphore_signal(
            barrier, inc=1, device_id={"layer": neighbour}, device_id_type=MESH
        )

    def remote(src, dst, send_sem, recv_sem, target):
        return pltpu.make_async_remote_copy(
            src_ref=src,
            dst_ref=dst,
            send_sem=send_sem,
            recv_sem=recv_sem,
            device_id={"layer": target},
            device_id_type=MESH,
        )

    def send_guess(q):
        return remote(gsend.at[q], shifted.at[q], g_sem.at[0, q], g_sem.at[1, q], right)

    def send_guess_over():
        return remote(gsend.at[0], guess_over, g_sem.at[0, 0], go_sem.at[0], n - 1)

    def forward_guess():
        return remote(guess_over, shifted.at[0], go_sem.at[1], g_sem.at[1, 0], 4)

    def send_coarse_over(g):
        slot = g - 1
        return remote(bbuf.at[g], rows_over.at[slot], cs_sem.at[g], ro_sem.at[0, slot], n - 2)

    def forward_coarse(g):
        slot = g - 1
        return remote(rows_over.at[slot], cin.at[g], ro_sem.at[1, slot], cr_sem.at[g], 4)

    def send_centre():
        return remote(wsend, wrecv, wx_sem.at[0], wx_sem.at[1], partner)

    def send_force():
        return remote(force, fo.at[core], fx_sem.at[0], fx_sem.at[1], partner)

    def first_coarse(g):
        src = out_ref.at[1, g]
        return remote(src, cin.at[g], cs_sem.at[g], cr_sem.at[g], 2 if n > 4 else n - 1)

    def send_coarse(g):
        return remote(bbuf.at[g], cin.at[g], cs_sem.at[g], cr_sem.at[g], runner_ahead)

    def send_fin(src, g):
        return remote(src.at[g], peer_fin.at[g], pf_sem.at[0, g], pf_sem.at[1, g], partner)

    def send_out(src, g):
        return remote(src.at[g], peer_out.at[g], po_sem.at[0, g], po_sem.at[1, g], partner)

    def cut(h):
        return slice(h * half, (h + 1) * half)

    band = side * images

    def build(h):
        for dx in range(3):
            piece = pad[1 : 1 + side, dx : dx + side, :, cut(h)]
            cols[h, band : band + rows, dx * half : (dx + 1) * half] = piece.reshape(
                rows, half
            ).astype(jnp.bfloat16)

    def taps_of(l, h, q):
        total = None
        for dy in range(3):
            window = cols[h, dy * band : dy * band + rows, :]
            block = wv[l, 3 * dy : 3 * dy + 3, h, :, cut(q)].reshape(3 * half, half)
            part = dot(window, block)
            total = part if total is None else total + part
        return total

    def fine(l, before, emit):
        before(0)
        build(0)
        parts = [taps_of(l, 0, q) for q in range(2)]
        before(1)
        build(1)
        for q in range(2):
            mixed = parts[q] + taps_of(l, 1, q) + b_ref[l : l + 1, cut(q)]
            base = pad[1 : 1 + side, 1 : 1 + side, :, cut(q)].reshape(rows, half)
            emit(q, base + step_size * jnp.tanh(mixed))

    def grid_of(value):
        return value.reshape(side, side, images, value.shape[-1])

    def to_pad(q, value):
        pad[1 : 1 + side, 1 : 1 + side, :, cut(q)] = grid_of(value)

    def coarse(field, centre, bias):
        mixed = dot(field.astype(jnp.bfloat16), centre) + bias
        return field + 2.0 * step_size * jnp.tanh(mixed)

    def no_wait(h):
        pass

    pad[...] = jnp.zeros_like(pad)
    for h in range(2):
        cols[h, 0:band, :] = jnp.zeros((band, 3 * half), jnp.bfloat16)
        cols[h, band + rows :, :] = jnp.zeros((band, 3 * half), jnp.bfloat16)
    get_images.wait()
    get_biases.wait()
    lanes = 128
    tiles = channels // lanes
    for m in range(images):
        for i in range(side):
            row = img_ref[m, i].astype(jnp.float32)
            for c in range(tiles):
                at = ((m * side + i) * tiles + c) * side
                stage[at : at + side, :] = row[:, c * lanes : (c + 1) * lanes]
    for i in range(side):
        for c in range(tiles):
            for j in range(side):
                at = (i * tiles + c) * side + j
                pad[1 + i, 1 + j, :, c * lanes : (c + 1) * lanes] = stage[
                    pl.ds(at, images, stride=side * tiles * side), :
                ]

    def first_layer(h):
        wait_load(0, h)
        start_load(1, h)

    fine(0, first_layer, to_pad)

    @pl.when(me == 0)
    def _():
        out_ref[0] = pad[1 : 1 + side, 1 : 1 + side]

    pl.semaphore_wait(barrier, len(distances))

    @pl.when(helps)
    def _():
        centre = wv[0, 4].reshape(channels, channels)
        wsend[0:channels, :] = centre.astype(jnp.float32)
        wsend[channels : channels + 8, :] = jnp.broadcast_to(b_ref[0:1, :], (8, channels))
        send_centre().start()

    @pl.when(runs)
    def _():
        wc[core] = wv[0, 4].reshape(channels, channels)
        bc[core] = jnp.broadcast_to(b_ref[0:1, :], (8, channels))

    def emit_guess(q, value):
        gsend[q] = value
        over = (me == 3) if forwards and q == 0 else False

        @pl.when(has_next & jnp.logical_not(over))
        def _():
            send_guess(q).start()

        if forwards and q == 0:

            @pl.when(over)
            def _():
                send_guess_over().start()

    fine(1, lambda h: wait_load(1, h), emit_guess)

    @pl.when(me == 0)
    def _():
        for q in range(2):
            out_ref[1, :, :, :, cut(q)] = grid_of(gsend[q])

    if forwards:

        @pl.when(me == n - 1)
        def _():
            send_guess_over().wait_recv()
            forward_guess().start()

    @pl.when(me >= 1)
    def _():
        def arrive(h):
            if h == 0:

                @pl.when(runs)
                def _():
                    send_centre().wait_recv()
                    wc[other] = wrecv[0:channels, :].astype(jnp.bfloat16)
                    bc[other] = wrecv[channels : channels + 8, :]

            else:

                @pl.when(me >= 2)
                def _():
                    centre_dot[...] = dot(shifted[0].astype(jnp.bfloat16), wv[0, 4, 0])

            send_guess(h).wait_recv()
            to_pad(h, shifted[h])

        fine(0, arrive, to_pad)

        @pl.when(me == 1)
        def _():
            out_ref[0] = pad[1 : 1 + side, 1 : 1 + side]

        def emit_end(q, value):
            out_ref[1, :, :, :, cut(q)] = grid_of(value)

        fine(1, no_wait, emit_end)

        @pl.when((me == 1) & has_next_pair)
        def _():
            for g in range(groups):
                first_coarse(g).start()

    def own_forcing():
        start = jnp.concatenate([shifted[0], shifted[1]], axis=1)
        rest = dot(shifted[1].astype(jnp.bfloat16), wv[0, 4, 1])
        mixed = centre_dot[...] + rest + b_ref[0:1, :]
        return out_ref[1] - grid_of(start + 2.0 * step_size * jnp.tanh(mixed))

    def emit_finished(q, value):
        out_ref[0, :, :, :, cut(q)] = grid_of(value)

    @pl.when(runs)
    def _():
        fo[core] = own_forcing()
        send_force().wait_recv()

        def advance(field, b, g):
            flat = field.reshape(side * images, channels)
            solved = coarse(flat, wc[b], bc[b, 0:1, :])
            return solved.reshape(side, images, channels) + fo[b, g]

        for g in range(groups):
            send_coarse(g).wait_recv()

            @pl.when(core == 1)
            def _():
                send_fin(cin, g).start()

            field = cin[g]
            first = advance(field, 0, g)
            abuf[g] = first
            second = advance(first, 1, g)
            bbuf[g] = second

            over = (me == 2) if forwards and g in (1, 2) else False

            @pl.when(has_next_pair & jnp.logical_not(over))
            def _():
                send_coarse(g).start()

            if forwards and g in (1, 2):

                @pl.when(over)
                def _():
                    send_coarse_over(g).start()

            @pl.when(has_next_pair)
            def _():
                send_fin(abuf, g).start()
                send_out(bbuf, g).start()

            @pl.when(core == 1)
            def _():
                send_out(abuf, g).start()

            pad[1 + g, 1 : 1 + side] = jnp.where(core == 0, field, first)
            out_ref[1, g] = jnp.where(core == 0, first, second)

        fine(0, no_wait, emit_finished)
        for g in range(groups):
            send_fin(cin, g).wait_send()
            send_out(abuf, g).wait_send()

            @pl.when(has_next_pair)
            def _():
                send_coarse(g).wait_send()

    @pl.when(helps)
    def _():
        force[...] = own_forcing()
        send_force().start()
        if forwards:

            @pl.when(me == n - 2)
            def _():
                for g in (1, 2):
                    send_coarse_over(g).wait_recv()
                    forward_coarse(g).start()

        for g in range(groups):
            send_fin(cin, g).wait_recv()
            pad[1 + g, 1 : 1 + side] = peer_fin[g]
        fine(0, no_wait, emit_finished)
        for g in range(groups):
            send_out(abuf, g).wait_recv()
            out_ref[1, g] = peer_out[g]
        send_centre().wait_send()
        send_force().wait_send()

    @pl.when(has_next)
    def _():
        for q in range(2):
            send_guess(q).wait_send()

    @pl.when((me == 1) & has_next_pair)
    def _():
        for g in range(groups):
            first_coarse(g).wait_send()

    if forwards:

        @pl.when(me == n - 1)
        def _():
            forward_guess().wait_send()

        @pl.when(me == n - 2)
        def _():
            for g in (1, 2):
                forward_coarse(g).wait_send()


def shards(n, images, weights, biases):
    count, side, _, channels = images.shape
    half = channels // 2
    rows = side * side * count
    groups = side
    piece = (groups, side, count, channels)
    taps = weights.reshape(2, 9, 2, half, channels)
    vmem = pl.BlockSpec(memory_space=pltpu.VMEM)
    hbm = pl.BlockSpec(memory_space=pl.ANY)
    f32, bf16 = jnp.float32, jnp.bfloat16
    out = pl.pallas_call(
        functools.partial(kernel, n),
        out_shape=pltpu.VMEM((2, side, side, count, channels), f32),
        in_specs=[hbm, hbm, hbm],
        out_specs=vmem,
        scratch_shapes=[
            pltpu.VMEM(images.shape, bf16),
            pltpu.VMEM(biases.shape, f32),
            pltpu.VMEM(taps.shape, bf16),
            pltpu.VMEM((side + 2, side + 2, count, channels), f32),
            pltpu.VMEM((2, rows + 2 * side * count, 3 * half), bf16),
            pltpu.VMEM((2, rows, half), f32),
            pltpu.VMEM((2, rows, half), f32),
            pltpu.VMEM((rows * channels // 128, 128), f32),
            pltpu.VMEM((rows, channels), f32),
            pltpu.VMEM((side, side, count, channels), f32),
            pltpu.VMEM((channels + 8, channels), f32),
            pltpu.VMEM((channels + 8, channels), f32),
            pltpu.VMEM((2, channels, channels), bf16),
            pltpu.VMEM((2, 8, channels), f32),
            pltpu.VMEM((2,) + piece, f32),
            pltpu.VMEM(piece, f32),
            pltpu.VMEM(piece, f32),
            pltpu.VMEM(piece, f32),
            pltpu.VMEM(piece, f32),
            pltpu.VMEM(piece, f32),
            pltpu.VMEM((rows, half), f32),
            pltpu.VMEM((2,) + piece[1:], f32),
            pltpu.SemaphoreType.DMA((2,)),
            pltpu.SemaphoreType.DMA((2, 2)),
            pltpu.SemaphoreType.DMA((2,)),
            pltpu.SemaphoreType.DMA((2, 2, 3)),
            pltpu.SemaphoreType.DMA((2, 2)),
            pltpu.SemaphoreType.DMA((2,)),
            pltpu.SemaphoreType.DMA((2,)),
            pltpu.SemaphoreType.DMA((groups,)),
            pltpu.SemaphoreType.DMA((groups,)),
            pltpu.SemaphoreType.DMA((2, groups)),
            pltpu.SemaphoreType.DMA((2, groups)),
        ],
        compiler_params=pltpu.CompilerParams(
            collective_id=0, has_side_effects=True, vmem_limit_bytes=56 * 2**20
        ),
    )(images, taps, biases)
    return jnp.transpose(out, (0, 3, 1, 2, 4))


def solution(mesh):
    return jax.shard_map(
        functools.partial(shards, mesh.shape["layer"]),
        mesh=mesh,
        in_specs=(P("batch", None, None, None), P("layer", None, None), P("layer", None)),
        out_specs=P("layer", "batch", None, None, None),
        check_vma=False,
    )
```

```python
import functools

import jax
import jax.numpy as jnp
from jax import lax
from jax.experimental import pallas as pl
from jax.experimental.pallas import tpu as pltpu
from jax.sharding import PartitionSpec as P

MESH = pl.DeviceIdType.MESH
step_size = 0.25


def dot(a, b):
    return jnp.dot(a, b, preferred_element_type=jnp.float32)


def kernel(
    n,
    img_hbm,
    w_hbm,
    b_hbm,
    out_ref,
    img_ref,
    b_ref,
    wv,
    pad,
    cols,
    gsend,
    shifted,
    stage,
    centre_dot,
    force,
    wsend,
    wrecv,
    wc,
    bc,
    fo,
    cin,
    abuf,
    bbuf,
    peer_fin,
    in_sem,
    w_sem,
    g_sem,
    wx_sem,
    fx_sem,
    cs_sem,
    cr_sem,
    pf_sem,
):
    me = lax.axis_index("layer")
    right = lax.rem(me + 1, n)
    images, side, _, channels = img_ref.shape
    half = channels // 2
    rows = side * side * images
    has_next = me < n - 1
    has_next_pair = me < n - 2
    core = lax.rem(me, 2)
    other = 1 - core
    partner = me + 1 - 2 * core
    runs = (me >= 2) & (core == jnp.where(has_next_pair, 0, 1))
    helps = (me >= 2) & (core == jnp.where(has_next_pair, 1, 0))
    runner_ahead = jnp.where(me == n - 4, n - 1, lax.rem(me + 2, n))
    groups = side

    def loads(l, h):
        return [
            pltpu.make_async_copy(
                w_hbm.at[l, 3 * r : 3 * r + 3, h],
                wv.at[l, 3 * r : 3 * r + 3, h],
                w_sem.at[l, h, r],
            )
            for r in range(3)
        ]

    def start_load(l, h):
        for copy in loads(l, h):
            copy.start()

    def wait_load(l, h):
        for copy in loads(l, h):
            copy.wait()

    get_images = pltpu.make_async_copy(img_hbm, img_ref, in_sem.at[0])
    get_biases = pltpu.make_async_copy(b_hbm, b_ref, in_sem.at[1])
    get_images.start()
    get_biases.start()
    start_load(0, 0)
    start_load(0, 1)

    barrier = pltpu.get_barrier_semaphore()
    for distance in (1, 2, 3, n - 3, n - 2, n - 1):
        neighbour = lax.rem(me + distance, n)
        pl.semaphore_signal(
            barrier, inc=1, device_id={"layer": neighbour}, device_id_type=MESH
        )

    def remote(src, dst, send_sem, recv_sem, target):
        return pltpu.make_async_remote_copy(
            src_ref=src,
            dst_ref=dst,
            send_sem=send_sem,
            recv_sem=recv_sem,
            device_id={"layer": target},
            device_id_type=MESH,
        )

    def send_guess(q):
        return remote(gsend.at[q], shifted.at[q], g_sem.at[0, q], g_sem.at[1, q], right)

    def send_centre():
        return remote(wsend, wrecv, wx_sem.at[0], wx_sem.at[1], partner)

    def send_force():
        return remote(force, fo.at[core], fx_sem.at[0], fx_sem.at[1], partner)

    def first_coarse(g):
        src = out_ref.at[1, g]
        return remote(src, cin.at[g], cs_sem.at[g], cr_sem.at[g], 2 if n > 4 else n - 1)

    def send_coarse(g):
        return remote(bbuf.at[g], cin.at[g], cs_sem.at[g], cr_sem.at[g], runner_ahead)

    def send_fin(src, g):
        return remote(src.at[g], peer_fin.at[g], pf_sem.at[0, g], pf_sem.at[1, g], partner)

    def cut(h):
        return slice(h * half, (h + 1) * half)

    band = side * images

    def build(h):
        for dx in range(3):
            piece = pad[1 : 1 + side, dx : dx + side, :, cut(h)]
            cols[h, band : band + rows, dx * half : (dx + 1) * half] = piece.reshape(
                rows, half
            ).astype(jnp.bfloat16)

    def taps_of(l, h, q):
        total = None
        for dy in range(3):
            window = cols[h, dy * band : dy * band + rows, :]
            block = wv[l, 3 * dy : 3 * dy + 3, h, :, cut(q)].reshape(3 * half, half)
            part = dot(window, block)
            total = part if total is None else total + part
        return total

    def fine(l, before, emit):
        before(0)
        build(0)
        parts = [taps_of(l, 0, q) for q in range(2)]
        before(1)
        build(1)
        for q in range(2):
            mixed = parts[q] + taps_of(l, 1, q) + b_ref[l : l + 1, cut(q)]
            base = pad[1 : 1 + side, 1 : 1 + side, :, cut(q)].reshape(rows, half)
            emit(q, base + step_size * jnp.tanh(mixed))

    def grid_of(value):
        return value.reshape(side, side, images, value.shape[-1])

    def to_pad(q, value):
        pad[1 : 1 + side, 1 : 1 + side, :, cut(q)] = grid_of(value)

    def coarse(field, centre, bias):
        mixed = dot(field.astype(jnp.bfloat16), centre) + bias
        return field + 2.0 * step_size * jnp.tanh(mixed)

    def no_wait(h):
        pass

    pad[...] = jnp.zeros_like(pad)
    for h in range(2):
        cols[h, 0:band, :] = jnp.zeros((band, 3 * half), jnp.bfloat16)
        cols[h, band + rows :, :] = jnp.zeros((band, 3 * half), jnp.bfloat16)
    get_images.wait()
    get_biases.wait()
    lanes = 128
    tiles = channels // lanes
    for m in range(images):
        for i in range(side):
            row = img_ref[m, i].astype(jnp.float32)
            for c in range(tiles):
                at = ((m * side + i) * tiles + c) * side
                stage[at : at + side, :] = row[:, c * lanes : (c + 1) * lanes]
    for i in range(side):
        for c in range(tiles):
            for j in range(side):
                at = (i * tiles + c) * side + j
                pad[1 + i, 1 + j, :, c * lanes : (c + 1) * lanes] = stage[
                    pl.ds(at, images, stride=side * tiles * side), :
                ]

    def first_layer(h):
        wait_load(0, h)
        start_load(1, h)

    fine(0, first_layer, to_pad)

    @pl.when(me == 0)
    def _():
        out_ref[0] = pad[1 : 1 + side, 1 : 1 + side]

    pl.semaphore_wait(barrier, 6)

    @pl.when(helps)
    def _():
        centre = wv[0, 4].reshape(channels, channels)
        wsend[0:channels, :] = centre.astype(jnp.float32)
        wsend[channels : channels + 8, :] = jnp.broadcast_to(b_ref[0:1, :], (8, channels))
        send_centre().start()

    @pl.when(runs)
    def _():
        wc[core] = wv[0, 4].reshape(channels, channels)
        bc[core] = jnp.broadcast_to(b_ref[0:1, :], (8, channels))

    def emit_guess(q, value):
        gsend[q] = value

        @pl.when(has_next)
        def _():
            send_guess(q).start()

    fine(1, lambda h: wait_load(1, h), emit_guess)

    @pl.when(me == 0)
    def _():
        for q in range(2):
            out_ref[1, :, :, :, cut(q)] = grid_of(gsend[q])

    @pl.when(me >= 1)
    def _():
        def arrive(h):
            if h == 0:

                @pl.when(runs)
                def _():
                    send_centre().wait_recv()
                    wc[other] = wrecv[0:channels, :].astype(jnp.bfloat16)
                    bc[other] = wrecv[channels : channels + 8, :]

            else:

                @pl.when(me >= 2)
                def _():
                    centre_dot[...] = dot(shifted[0].astype(jnp.bfloat16), wv[0, 4, 0])

            send_guess(h).wait_recv()
            to_pad(h, shifted[h])

        fine(0, arrive, to_pad)

        @pl.when(me == 1)
        def _():
            out_ref[0] = pad[1 : 1 + side, 1 : 1 + side]

        def emit_end(q, value):
            out_ref[1, :, :, :, cut(q)] = grid_of(value)

        fine(1, no_wait, emit_end)

        @pl.when((me == 1) & has_next_pair)
        def _():
            for g in range(groups):
                first_coarse(g).start()

    def own_forcing():
        start = jnp.concatenate([shifted[0], shifted[1]], axis=1)
        rest = dot(shifted[1].astype(jnp.bfloat16), wv[0, 4, 1])
        mixed = centre_dot[...] + rest + b_ref[0:1, :]
        return out_ref[1] - grid_of(start + 2.0 * step_size * jnp.tanh(mixed))

    def emit_finished(q, value):
        out_ref[0, :, :, :, cut(q)] = grid_of(value)

    @pl.when(runs)
    def _():
        fo[core] = own_forcing()
        send_force().wait_recv()

        def advance(field, b, g):
            flat = field.reshape(side * images, channels)
            solved = coarse(flat, wc[b], bc[b, 0:1, :])
            return solved.reshape(side, images, channels) + fo[b, g]

        for g in range(groups):
            send_coarse(g).wait_recv()

            @pl.when(core == 1)
            def _():
                send_fin(cin, g).start()

            field = cin[g]
            first = advance(field, 0, g)
            abuf[g] = first
            second = advance(first, 1, g)
            bbuf[g] = second

            @pl.when(has_next_pair)
            def _():
                send_coarse(g).start()

            pad[1 + g, 1 : 1 + side] = jnp.where(core == 0, field, first)
            out_ref[1, g] = jnp.where(core == 0, first, second)

        @pl.when(has_next_pair)
        def _():
            for g in range(groups):
                send_fin(abuf, g).start()

        fine(0, no_wait, emit_finished)
        for g in range(groups):
            send_fin(cin, g).wait_send()

            @pl.when(has_next_pair)
            def _():
                send_coarse(g).wait_send()

    @pl.when(helps)
    def _():
        force[...] = own_forcing()
        send_force().start()
        for g in range(groups):
            send_fin(cin, g).wait_recv()
            pad[1 + g, 1 : 1 + side] = peer_fin[g]
        fine(0, no_wait, emit_finished)
        entry = peer_fin[...].reshape(rows, channels)
        centre = wv[0, 4].reshape(channels, channels)
        out_ref[1] = grid_of(coarse(entry, centre, b_ref[0:1, :])) + force[...]
        send_centre().wait_send()
        send_force().wait_send()

    @pl.when(has_next)
    def _():
        for q in range(2):
            send_guess(q).wait_send()

    @pl.when((me == 1) & has_next_pair)
    def _():
        for g in range(groups):
            first_coarse(g).wait_send()


def shards(n, images, weights, biases):
    count, side, _, channels = images.shape
    half = channels // 2
    rows = side * side * count
    groups = side
    piece = (groups, side, count, channels)
    taps = weights.reshape(2, 9, 2, half, channels)
    vmem = pl.BlockSpec(memory_space=pltpu.VMEM)
    hbm = pl.BlockSpec(memory_space=pl.ANY)
    f32, bf16 = jnp.float32, jnp.bfloat16
    out = pl.pallas_call(
        functools.partial(kernel, n),
        out_shape=pltpu.VMEM((2, side, side, count, channels), f32),
        in_specs=[hbm, hbm, hbm],
        out_specs=vmem,
        scratch_shapes=[
            pltpu.VMEM(images.shape, bf16),
            pltpu.VMEM(biases.shape, f32),
            pltpu.VMEM(taps.shape, bf16),
            pltpu.VMEM((side + 2, side + 2, count, channels), f32),
            pltpu.VMEM((2, rows + 2 * side * count, 3 * half), bf16),
            pltpu.VMEM((2, rows, half), f32),
            pltpu.VMEM((2, rows, half), f32),
            pltpu.VMEM((rows * channels // 128, 128), f32),
            pltpu.VMEM((rows, channels), f32),
            pltpu.VMEM((side, side, count, channels), f32),
            pltpu.VMEM((channels + 8, channels), f32),
            pltpu.VMEM((channels + 8, channels), f32),
            pltpu.VMEM((2, channels, channels), bf16),
            pltpu.VMEM((2, 8, channels), f32),
            pltpu.VMEM((2,) + piece, f32),
            pltpu.VMEM(piece, f32),
            pltpu.VMEM(piece, f32),
            pltpu.VMEM(piece, f32),
            pltpu.VMEM(piece, f32),
            pltpu.SemaphoreType.DMA((2,)),
            pltpu.SemaphoreType.DMA((2, 2, 3)),
            pltpu.SemaphoreType.DMA((2, 2)),
            pltpu.SemaphoreType.DMA((2,)),
            pltpu.SemaphoreType.DMA((2,)),
            pltpu.SemaphoreType.DMA((groups,)),
            pltpu.SemaphoreType.DMA((groups,)),
            pltpu.SemaphoreType.DMA((2, groups)),
        ],
        compiler_params=pltpu.CompilerParams(
            collective_id=0, has_side_effects=True, vmem_limit_bytes=56 * 2**20
        ),
    )(images, taps, biases)
    return jnp.transpose(out, (0, 3, 1, 2, 4))


def solution(mesh):
    return jax.shard_map(
        functools.partial(shards, mesh.shape["layer"]),
        mesh=mesh,
        in_specs=(P("batch", None, None, None), P("layer", None, None), P("layer", None)),
        out_specs=P("layer", "batch", None, None, None),
        check_vma=False,
    )
```

```python
import functools

import jax
import jax.numpy as jnp
from jax import lax
from jax.experimental import pallas as pl
from jax.experimental.pallas import tpu as pltpu
from jax.sharding import PartitionSpec as P

MESH = pl.DeviceIdType.MESH
step_size = 0.25


def dot(a, b):
    return jnp.dot(a, b, preferred_element_type=jnp.float32)


def kernel(
    n,
    img_hbm,
    w_hbm,
    b_hbm,
    out_ref,
    img_ref,
    b_ref,
    wv,
    pad,
    cols,
    gsend,
    shifted,
    stage,
    centre_dot,
    force,
    wsend,
    wrecv,
    wc,
    bc,
    fo,
    cin,
    abuf,
    bbuf,
    peer_fin,
    in_sem,
    w_sem,
    g_sem,
    wx_sem,
    fx_sem,
    cs_sem,
    cr_sem,
    pf_sem,
):
    me = lax.axis_index("layer")
    right = lax.rem(me + 1, n)
    images, side, _, channels = img_ref.shape
    half = channels // 2
    rows = side * side * images
    has_next = me < n - 1
    has_next_pair = me < n - 2
    core = lax.rem(me, 2)
    other = 1 - core
    partner = me + 1 - 2 * core
    runs = (me >= 2) & (core == jnp.where(has_next_pair, 0, 1))
    helps = (me >= 2) & (core == jnp.where(has_next_pair, 1, 0))
    runner_ahead = jnp.where(me == n - 4, n - 1, lax.rem(me + 2, n))
    groups = side

    def loads(l, h):
        return [
            pltpu.make_async_copy(
                w_hbm.at[l, 3 * r : 3 * r + 3, h],
                wv.at[l, 3 * r : 3 * r + 3, h],
                w_sem.at[l, h, r],
            )
            for r in range(3)
        ]

    def start_load(l, h):
        for copy in loads(l, h):
            copy.start()

    def wait_load(l, h):
        for copy in loads(l, h):
            copy.wait()

    get_images = pltpu.make_async_copy(img_hbm, img_ref, in_sem.at[0])
    get_biases = pltpu.make_async_copy(b_hbm, b_ref, in_sem.at[1])
    get_images.start()
    get_biases.start()
    for l in range(2):
        for h in range(2):
            start_load(l, h)

    barrier = pltpu.get_barrier_semaphore()
    for distance in (1, 2, 3, n - 3, n - 2, n - 1):
        neighbour = lax.rem(me + distance, n)
        pl.semaphore_signal(
            barrier, inc=1, device_id={"layer": neighbour}, device_id_type=MESH
        )

    def remote(src, dst, send_sem, recv_sem, target):
        return pltpu.make_async_remote_copy(
            src_ref=src,
            dst_ref=dst,
            send_sem=send_sem,
            recv_sem=recv_sem,
            device_id={"layer": target},
            device_id_type=MESH,
        )

    def send_guess(q):
        return remote(gsend.at[q], shifted.at[q], g_sem.at[0, q], g_sem.at[1, q], right)

    def send_centre():
        return remote(wsend, wrecv, wx_sem.at[0], wx_sem.at[1], partner)

    def send_force():
        return remote(force, fo.at[core], fx_sem.at[0], fx_sem.at[1], partner)

    def first_coarse(g):
        src = out_ref.at[1, g]
        return remote(src, cin.at[g], cs_sem.at[g], cr_sem.at[g], 2 if n > 4 else n - 1)

    def send_coarse(g):
        return remote(bbuf.at[g], cin.at[g], cs_sem.at[g], cr_sem.at[g], runner_ahead)

    def send_fin(src, g):
        return remote(src.at[g], peer_fin.at[g], pf_sem.at[0, g], pf_sem.at[1, g], partner)

    def cut(h):
        return slice(h * half, (h + 1) * half)

    band = side * images

    def build(h):
        for dx in range(3):
            piece = pad[1 : 1 + side, dx : dx + side, :, cut(h)]
            cols[h, band : band + rows, dx * half : (dx + 1) * half] = piece.reshape(
                rows, half
            ).astype(jnp.bfloat16)

    def taps_of(l, h, q):
        total = None
        for dy in range(3):
            window = cols[h, dy * band : dy * band + rows, :]
            block = wv[l, 3 * dy : 3 * dy + 3, h, :, cut(q)].reshape(3 * half, half)
            part = dot(window, block)
            total = part if total is None else total + part
        return total

    def fine(l, before, emit):
        before(0)
        build(0)
        parts = [taps_of(l, 0, q) for q in range(2)]
        before(1)
        build(1)
        for q in range(2):
            mixed = parts[q] + taps_of(l, 1, q) + b_ref[l : l + 1, cut(q)]
            base = pad[1 : 1 + side, 1 : 1 + side, :, cut(q)].reshape(rows, half)
            emit(q, base + step_size * jnp.tanh(mixed))

    def grid_of(value):
        return value.reshape(side, side, images, value.shape[-1])

    def to_pad(q, value):
        pad[1 : 1 + side, 1 : 1 + side, :, cut(q)] = grid_of(value)

    def coarse(field, centre, bias):
        mixed = dot(field.astype(jnp.bfloat16), centre) + bias
        return field + 2.0 * step_size * jnp.tanh(mixed)

    def no_wait(h):
        pass

    pad[...] = jnp.zeros_like(pad)
    for h in range(2):
        cols[h, 0:band, :] = jnp.zeros((band, 3 * half), jnp.bfloat16)
        cols[h, band + rows :, :] = jnp.zeros((band, 3 * half), jnp.bfloat16)
    get_images.wait()
    get_biases.wait()
    lanes = 128
    tiles = channels // lanes
    for m in range(images):
        for i in range(side):
            row = img_ref[m, i].astype(jnp.float32)
            for c in range(tiles):
                at = ((m * side + i) * tiles + c) * side
                stage[at : at + side, :] = row[:, c * lanes : (c + 1) * lanes]
    for i in range(side):
        for c in range(tiles):
            for j in range(side):
                at = (i * tiles + c) * side + j
                pad[1 + i, 1 + j, :, c * lanes : (c + 1) * lanes] = stage[
                    pl.ds(at, images, stride=side * tiles * side), :
                ]

    fine(0, lambda h: wait_load(0, h), to_pad)

    @pl.when(me == 0)
    def _():
        out_ref[0] = pad[1 : 1 + side, 1 : 1 + side]

    pl.semaphore_wait(barrier, 6)

    @pl.when(helps)
    def _():
        centre = wv[0, 4].reshape(channels, channels)
        wsend[0:channels, :] = centre.astype(jnp.float32)
        wsend[channels : channels + 8, :] = jnp.broadcast_to(b_ref[0:1, :], (8, channels))
        send_centre().start()

    @pl.when(runs)
    def _():
        wc[core] = wv[0, 4].reshape(channels, channels)
        bc[core] = jnp.broadcast_to(b_ref[0:1, :], (8, channels))

    def emit_guess(q, value):
        gsend[q] = value

        @pl.when(has_next)
        def _():
            send_guess(q).start()

    fine(1, lambda h: wait_load(1, h), emit_guess)

    @pl.when(me == 0)
    def _():
        for q in range(2):
            out_ref[1, :, :, :, cut(q)] = grid_of(gsend[q])

    @pl.when(me >= 1)
    def _():
        def arrive(h):
            if h == 0:

                @pl.when(runs)
                def _():
                    send_centre().wait_recv()
                    wc[other] = wrecv[0:channels, :].astype(jnp.bfloat16)
                    bc[other] = wrecv[channels : channels + 8, :]

            else:

                @pl.when(me >= 2)
                def _():
                    centre_dot[...] = dot(shifted[0].astype(jnp.bfloat16), wv[0, 4, 0])

            send_guess(h).wait_recv()
            to_pad(h, shifted[h])

        fine(0, arrive, to_pad)

        @pl.when(me == 1)
        def _():
            out_ref[0] = pad[1 : 1 + side, 1 : 1 + side]

        def emit_end(q, value):
            out_ref[1, :, :, :, cut(q)] = grid_of(value)

        fine(1, no_wait, emit_end)

        @pl.when((me == 1) & has_next_pair)
        def _():
            for g in range(groups):
                first_coarse(g).start()

    def own_forcing():
        start = jnp.concatenate([shifted[0], shifted[1]], axis=1)
        rest = dot(shifted[1].astype(jnp.bfloat16), wv[0, 4, 1])
        mixed = centre_dot[...] + rest + b_ref[0:1, :]
        return out_ref[1] - grid_of(start + 2.0 * step_size * jnp.tanh(mixed))

    def emit_finished(q, value):
        out_ref[0, :, :, :, cut(q)] = grid_of(value)

    @pl.when(runs)
    def _():
        fo[core] = own_forcing()
        send_force().wait_recv()

        def advance(field, b, g):
            flat = field.reshape(side * images, channels)
            solved = coarse(flat, wc[b], bc[b, 0:1, :])
            return solved.reshape(side, images, channels) + fo[b, g]

        for g in range(groups):
            send_coarse(g).wait_recv()

            @pl.when(core == 1)
            def _():
                send_fin(cin, g).start()

            field = cin[g]
            first = advance(field, 0, g)
            abuf[g] = first
            second = advance(first, 1, g)
            bbuf[g] = second

            @pl.when(has_next_pair)
            def _():
                send_coarse(g).start()

            pad[1 + g, 1 : 1 + side] = jnp.where(core == 0, field, first)
            out_ref[1, g] = jnp.where(core == 0, first, second)

        @pl.when(has_next_pair)
        def _():
            for g in range(groups):
                send_fin(abuf, g).start()

        fine(0, no_wait, emit_finished)
        for g in range(groups):
            send_fin(cin, g).wait_send()

            @pl.when(has_next_pair)
            def _():
                send_coarse(g).wait_send()

    @pl.when(helps)
    def _():
        force[...] = own_forcing()
        send_force().start()
        for g in range(groups):
            send_fin(cin, g).wait_recv()
            pad[1 + g, 1 : 1 + side] = peer_fin[g]
        fine(0, no_wait, emit_finished)
        entry = peer_fin[...].reshape(rows, channels)
        centre = wv[0, 4].reshape(channels, channels)
        out_ref[1] = grid_of(coarse(entry, centre, b_ref[0:1, :])) + force[...]
        send_centre().wait_send()
        send_force().wait_send()

    @pl.when(has_next)
    def _():
        for q in range(2):
            send_guess(q).wait_send()

    @pl.when((me == 1) & has_next_pair)
    def _():
        for g in range(groups):
            first_coarse(g).wait_send()


def shards(n, images, weights, biases):
    count, side, _, channels = images.shape
    half = channels // 2
    rows = side * side * count
    groups = side
    piece = (groups, side, count, channels)
    taps = weights.reshape(2, 9, 2, half, channels)
    vmem = pl.BlockSpec(memory_space=pltpu.VMEM)
    hbm = pl.BlockSpec(memory_space=pl.ANY)
    f32, bf16 = jnp.float32, jnp.bfloat16
    out = pl.pallas_call(
        functools.partial(kernel, n),
        out_shape=pltpu.VMEM((2, side, side, count, channels), f32),
        in_specs=[hbm, hbm, hbm],
        out_specs=vmem,
        scratch_shapes=[
            pltpu.VMEM(images.shape, bf16),
            pltpu.VMEM(biases.shape, f32),
            pltpu.VMEM(taps.shape, bf16),
            pltpu.VMEM((side + 2, side + 2, count, channels), f32),
            pltpu.VMEM((2, rows + 2 * side * count, 3 * half), bf16),
            pltpu.VMEM((2, rows, half), f32),
            pltpu.VMEM((2, rows, half), f32),
            pltpu.VMEM((rows * channels // 128, 128), f32),
            pltpu.VMEM((rows, channels), f32),
            pltpu.VMEM((side, side, count, channels), f32),
            pltpu.VMEM((channels + 8, channels), f32),
            pltpu.VMEM((channels + 8, channels), f32),
            pltpu.VMEM((2, channels, channels), bf16),
            pltpu.VMEM((2, 8, channels), f32),
            pltpu.VMEM((2,) + piece, f32),
            pltpu.VMEM(piece, f32),
            pltpu.VMEM(piece, f32),
            pltpu.VMEM(piece, f32),
            pltpu.VMEM(piece, f32),
            pltpu.SemaphoreType.DMA((2,)),
            pltpu.SemaphoreType.DMA((2, 2, 3)),
            pltpu.SemaphoreType.DMA((2, 2)),
            pltpu.SemaphoreType.DMA((2,)),
            pltpu.SemaphoreType.DMA((2,)),
            pltpu.SemaphoreType.DMA((groups,)),
            pltpu.SemaphoreType.DMA((groups,)),
            pltpu.SemaphoreType.DMA((2, groups)),
        ],
        compiler_params=pltpu.CompilerParams(
            collective_id=0, has_side_effects=True, vmem_limit_bytes=56 * 2**20
        ),
    )(images, taps, biases)
    return jnp.transpose(out, (0, 3, 1, 2, 4))


def solution(mesh):
    return jax.shard_map(
        functools.partial(shards, mesh.shape["layer"]),
        mesh=mesh,
        in_specs=(P("batch", None, None, None), P("layer", None, None), P("layer", None)),
        out_specs=P("layer", "batch", None, None, None),
        check_vma=False,
    )
```

```python
import functools

import jax
import jax.numpy as jnp
from jax import lax
from jax.experimental import pallas as pl
from jax.experimental.pallas import tpu as pltpu
from jax.sharding import PartitionSpec as P

MESH = pl.DeviceIdType.MESH
step_size = 0.25


def dot(a, b):
    return jnp.dot(a, b, preferred_element_type=jnp.float32)


def kernel(
    n,
    img_hbm,
    w_hbm,
    b_hbm,
    out_ref,
    img_ref,
    b_ref,
    wv,
    pad,
    cols,
    gsend,
    shifted,
    stage,
    centre_dot,
    force,
    wsend,
    wrecv,
    wc,
    bc,
    fo,
    cin,
    abuf,
    bbuf,
    peer_fin,
    in_sem,
    w_sem,
    g_sem,
    wx_sem,
    fx_sem,
    cs_sem,
    cr_sem,
    pf_sem,
):
    me = lax.axis_index("layer")
    right = lax.rem(me + 1, n)
    images, side, _, channels = img_ref.shape
    half = channels // 2
    rows = side * side * images
    has_next = me < n - 1
    has_next_pair = me < n - 2
    core = lax.rem(me, 2)
    other = 1 - core
    partner = me + 1 - 2 * core
    runs = (me >= 2) & (core == jnp.where(has_next_pair, 0, 1))
    helps = (me >= 2) & (core == jnp.where(has_next_pair, 1, 0))
    runner_ahead = jnp.where(me == n - 4, n - 1, lax.rem(me + 2, n))
    groups = side

    def loads(l, h):
        return [
            pltpu.make_async_copy(
                w_hbm.at[l, 3 * r : 3 * r + 3, h],
                wv.at[l, 3 * r : 3 * r + 3, h],
                w_sem.at[l, h, r],
            )
            for r in range(3)
        ]

    def start_load(l, h):
        for copy in loads(l, h):
            copy.start()

    def wait_load(l, h):
        for copy in loads(l, h):
            copy.wait()

    get_images = pltpu.make_async_copy(img_hbm, img_ref, in_sem.at[0])
    get_biases = pltpu.make_async_copy(b_hbm, b_ref, in_sem.at[1])
    get_images.start()
    get_biases.start()
    for l in range(2):
        for h in range(2):
            start_load(l, h)

    barrier = pltpu.get_barrier_semaphore()
    for distance in (1, 2, 3, n - 3, n - 2, n - 1):
        neighbour = lax.rem(me + distance, n)
        pl.semaphore_signal(
            barrier, inc=1, device_id={"layer": neighbour}, device_id_type=MESH
        )

    def remote(src, dst, send_sem, recv_sem, target):
        return pltpu.make_async_remote_copy(
            src_ref=src,
            dst_ref=dst,
            send_sem=send_sem,
            recv_sem=recv_sem,
            device_id={"layer": target},
            device_id_type=MESH,
        )

    def send_guess(q):
        return remote(gsend.at[q], shifted.at[q], g_sem.at[0, q], g_sem.at[1, q], right)

    def send_centre():
        return remote(wsend, wrecv, wx_sem.at[0], wx_sem.at[1], partner)

    def send_force():
        return remote(force, fo.at[core], fx_sem.at[0], fx_sem.at[1], partner)

    def first_coarse(g):
        src = out_ref.at[1, g]
        return remote(src, cin.at[g], cs_sem.at[g], cr_sem.at[g], 2 if n > 4 else n - 1)

    def send_coarse(g):
        return remote(bbuf.at[g], cin.at[g], cs_sem.at[g], cr_sem.at[g], runner_ahead)

    def send_fin(src, g):
        return remote(src.at[g], peer_fin.at[g], pf_sem.at[0, g], pf_sem.at[1, g], partner)

    def cut(h):
        return slice(h * half, (h + 1) * half)

    band = side * images

    def build(h):
        for dx in range(3):
            piece = pad[1 : 1 + side, dx : dx + side, :, cut(h)]
            cols[h, band : band + rows, dx * half : (dx + 1) * half] = piece.reshape(
                rows, half
            ).astype(jnp.bfloat16)

    def taps_of(l, h, q):
        total = None
        for dy in range(3):
            window = cols[h, dy * band : dy * band + rows, :]
            block = wv[l, 3 * dy : 3 * dy + 3, h, :, cut(q)].reshape(3 * half, half)
            part = dot(window, block)
            total = part if total is None else total + part
        return total

    def fine(l, before, emit):
        before(0)
        build(0)
        parts = [taps_of(l, 0, q) for q in range(2)]
        before(1)
        build(1)
        for q in range(2):
            mixed = parts[q] + taps_of(l, 1, q) + b_ref[l : l + 1, cut(q)]
            base = pad[1 : 1 + side, 1 : 1 + side, :, cut(q)].reshape(rows, half)
            emit(q, base + step_size * jnp.tanh(mixed))

    def grid_of(value):
        return value.reshape(side, side, images, value.shape[-1])

    def to_pad(q, value):
        pad[1 : 1 + side, 1 : 1 + side, :, cut(q)] = grid_of(value)

    def coarse(field, centre, bias):
        mixed = dot(field.astype(jnp.bfloat16), centre) + bias
        return field + 2.0 * step_size * jnp.tanh(mixed)

    def no_wait(h):
        pass

    pad[...] = jnp.zeros_like(pad)
    for h in range(2):
        cols[h, 0:band, :] = jnp.zeros((band, 3 * half), jnp.bfloat16)
        cols[h, band + rows :, :] = jnp.zeros((band, 3 * half), jnp.bfloat16)
    get_images.wait()
    get_biases.wait()
    lanes = 128
    tiles = channels // lanes
    for m in range(images):
        for i in range(side):
            row = img_ref[m, i].astype(jnp.float32)
            for c in range(tiles):
                at = ((m * side + i) * tiles + c) * side
                stage[at : at + side, :] = row[:, c * lanes : (c + 1) * lanes]
    for i in range(side):
        for c in range(tiles):
            for j in range(side):
                at = (i * tiles + c) * side + j
                pad[1 + i, 1 + j, :, c * lanes : (c + 1) * lanes] = stage[
                    pl.ds(at, images, stride=side * tiles * side), :
                ]

    fine(0, lambda h: wait_load(0, h), to_pad)

    @pl.when(me == 0)
    def _():
        out_ref[0] = pad[1 : 1 + side, 1 : 1 + side]

    pl.semaphore_wait(barrier, 6)

    @pl.when(helps)
    def _():
        centre = wv[0, 4].reshape(channels, channels)
        wsend[0:channels, :] = centre.astype(jnp.float32)
        wsend[channels : channels + 8, :] = jnp.broadcast_to(b_ref[0:1, :], (8, channels))
        send_centre().start()

    @pl.when(runs)
    def _():
        wc[core] = wv[0, 4].reshape(channels, channels)
        bc[core] = jnp.broadcast_to(b_ref[0:1, :], (8, channels))

    def emit_guess(q, value):
        gsend[q] = value

        @pl.when(has_next)
        def _():
            send_guess(q).start()

    fine(1, lambda h: wait_load(1, h), emit_guess)

    @pl.when(me == 0)
    def _():
        for q in range(2):
            out_ref[1, :, :, :, cut(q)] = grid_of(gsend[q])

    @pl.when(me >= 1)
    def _():
        def arrive(h):
            if h == 0:

                @pl.when(runs)
                def _():
                    send_centre().wait_recv()
                    wc[other] = wrecv[0:channels, :].astype(jnp.bfloat16)
                    bc[other] = wrecv[channels : channels + 8, :]

            else:

                @pl.when(me >= 2)
                def _():
                    centre_dot[...] = dot(shifted[0].astype(jnp.bfloat16), wv[0, 4, 0])

            send_guess(h).wait_recv()
            to_pad(h, shifted[h])

        fine(0, arrive, to_pad)

        @pl.when(me == 1)
        def _():
            out_ref[0] = pad[1 : 1 + side, 1 : 1 + side]

        def emit_end(q, value):
            out_ref[1, :, :, :, cut(q)] = grid_of(value)

        fine(1, no_wait, emit_end)

        @pl.when((me == 1) & has_next_pair)
        def _():
            for g in range(groups):
                first_coarse(g).start()

    def own_forcing():
        start = jnp.concatenate([shifted[0], shifted[1]], axis=1)
        rest = dot(shifted[1].astype(jnp.bfloat16), wv[0, 4, 1])
        mixed = centre_dot[...] + rest + b_ref[0:1, :]
        return out_ref[1] - grid_of(start + 2.0 * step_size * jnp.tanh(mixed))

    def emit_finished(q, value):
        out_ref[0, :, :, :, cut(q)] = grid_of(value)

    @pl.when(runs)
    def _():
        fo[core] = own_forcing()
        send_force().wait_recv()

        def advance(field, b, g):
            flat = field.reshape(2 * side * images, channels)
            solved = coarse(flat, wc[b], bc[b, 0:1, :])
            return solved.reshape(2, side, images, channels) + fo[b, g : g + 2]

        for g in range(0, groups, 2):
            for r in (g, g + 1):
                send_coarse(r).wait_recv()

            @pl.when(core == 1)
            def _():
                for r in (g, g + 1):
                    send_fin(cin, r).start()

            field = cin[g : g + 2]
            first = advance(field, 0, g)
            abuf[g : g + 2] = first
            second = advance(first, 1, g)
            bbuf[g : g + 2] = second

            @pl.when(has_next_pair)
            def _():
                for r in (g, g + 1):
                    send_coarse(r).start()

            pad[1 + g : 3 + g, 1 : 1 + side] = jnp.where(core == 0, field, first)
            out_ref[1, g : g + 2] = jnp.where(core == 0, first, second)

        @pl.when(has_next_pair)
        def _():
            for g in range(groups):
                send_fin(abuf, g).start()

        fine(0, no_wait, emit_finished)
        for g in range(groups):
            send_fin(cin, g).wait_send()

            @pl.when(has_next_pair)
            def _():
                send_coarse(g).wait_send()

    @pl.when(helps)
    def _():
        force[...] = own_forcing()
        send_force().start()
        for g in range(groups):
            send_fin(cin, g).wait_recv()
            pad[1 + g, 1 : 1 + side] = peer_fin[g]
        fine(0, no_wait, emit_finished)
        entry = peer_fin[...].reshape(rows, channels)
        centre = wv[0, 4].reshape(channels, channels)
        out_ref[1] = grid_of(coarse(entry, centre, b_ref[0:1, :])) + force[...]
        send_centre().wait_send()
        send_force().wait_send()

    @pl.when(has_next)
    def _():
        for q in range(2):
            send_guess(q).wait_send()

    @pl.when((me == 1) & has_next_pair)
    def _():
        for g in range(groups):
            first_coarse(g).wait_send()


def shards(n, images, weights, biases):
    count, side, _, channels = images.shape
    half = channels // 2
    rows = side * side * count
    groups = side
    piece = (groups, side, count, channels)
    taps = weights.reshape(2, 9, 2, half, channels)
    vmem = pl.BlockSpec(memory_space=pltpu.VMEM)
    hbm = pl.BlockSpec(memory_space=pl.ANY)
    f32, bf16 = jnp.float32, jnp.bfloat16
    out = pl.pallas_call(
        functools.partial(kernel, n),
        out_shape=pltpu.VMEM((2, side, side, count, channels), f32),
        in_specs=[hbm, hbm, hbm],
        out_specs=vmem,
        scratch_shapes=[
            pltpu.VMEM(images.shape, bf16),
            pltpu.VMEM(biases.shape, f32),
            pltpu.VMEM(taps.shape, bf16),
            pltpu.VMEM((side + 2, side + 2, count, channels), f32),
            pltpu.VMEM((2, rows + 2 * side * count, 3 * half), bf16),
            pltpu.VMEM((2, rows, half), f32),
            pltpu.VMEM((2, rows, half), f32),
            pltpu.VMEM((rows * channels // 128, 128), f32),
            pltpu.VMEM((rows, channels), f32),
            pltpu.VMEM((side, side, count, channels), f32),
            pltpu.VMEM((channels + 8, channels), f32),
            pltpu.VMEM((channels + 8, channels), f32),
            pltpu.VMEM((2, channels, channels), bf16),
            pltpu.VMEM((2, 8, channels), f32),
            pltpu.VMEM((2,) + piece, f32),
            pltpu.VMEM(piece, f32),
            pltpu.VMEM(piece, f32),
            pltpu.VMEM(piece, f32),
            pltpu.VMEM(piece, f32),
            pltpu.SemaphoreType.DMA((2,)),
            pltpu.SemaphoreType.DMA((2, 2, 3)),
            pltpu.SemaphoreType.DMA((2, 2)),
            pltpu.SemaphoreType.DMA((2,)),
            pltpu.SemaphoreType.DMA((2,)),
            pltpu.SemaphoreType.DMA((groups,)),
            pltpu.SemaphoreType.DMA((groups,)),
            pltpu.SemaphoreType.DMA((2, groups)),
        ],
        compiler_params=pltpu.CompilerParams(
            collective_id=0, has_side_effects=True, vmem_limit_bytes=56 * 2**20
        ),
    )(images, taps, biases)
    return jnp.transpose(out, (0, 3, 1, 2, 4))


def solution(mesh):
    return jax.shard_map(
        functools.partial(shards, mesh.shape["layer"]),
        mesh=mesh,
        in_specs=(P("batch", None, None, None), P("layer", None, None), P("layer", None)),
        out_specs=P("layer", "batch", None, None, None),
        check_vma=False,
    )
```
